256 devices in a mesh: role: 2 (over core), grp: 4 (over x), dev: 32 (over z, y).
Axes of the slice: x: 4, y: 4, z: 8, core: 2. Of those that a mesh axis runs over, the one named last changes fastest.
Arguments:
- pool_pages: bfloat16 [2, 4, 32, 24, 64, 576], P('role', 'grp', 'dev'), may hold values from -8 to 8
- kv_gain: float32 [512], replicated, may hold values from 0.25 to 1.75
- queries: bfloat16 [48, 4, 128, 576], P('grp', None, ('role', 'dev')), may hold values from -64 to 64
- decode_latent: bfloat16 [48, 4, 576], P('grp'), may hold values from -8 to 8
- served_request: int32 [48], replicated, may hold values from 0 to 47, each once
- resident_pages: int32 [4, 12], P('grp'), may hold values from 1 to 384, 768 in all within a row
- resident_tail: int32 [4, 12], P('grp'), may hold values from 1 to 64
- page_dest: int32 [4, 32, 24], P('grp'), may hold values from 0 to 63, as said below
Outputs:
- attention: bfloat16 [48, 4, 128, 512], P('grp', None, ('role', 'dev'))
- received_cache: bfloat16 [4, 32, 64, 64, 576], P('grp', 'dev')
The draws below stay inside these ranges and needn't reach their ends.
Inputs may be any that keep to these rules, and one draw needn't show every extreme that they name: `page_dest`: within each group and prefill device the values are distinct. At most 2 pages of one prefill device go to one owner; in each group one owner receives exactly 2 pages from every prefill device. `resident_pages`: the counts of each group sum to 768. `served_request`: each request appears once.
All inputs are finite; a program needn't handle non-finite values.
Results may differ from the reference program's by a relative error of at most 0.0015.
The reference program's roundings to bfloat16 on the way count: a program that leaves them out, or rounds other values in their place, can miss the bound.
Values may be sent and summed in bfloat16 or wider, within the bound.
A program may use at most 128 MiB of HBM per device.

```python
import math
import jax
import jax.numpy as jnp
import numpy as np
from jax import lax

HEADS = 128
LAT = 512
ROPE = 64
KDIM = 576
PAGE = 64
STEPS = 4
SPAN_PAGES = 2
REQ_GRP = 12
GROUPS = 4
OWNERS = 32
REQUESTS = 48
PAGES_DEV = 24
CAP = 2
SPAN = 4096
RES_TOTAL = 768
RES_MOST = 384
N_ROLE = 2


def shared_parts(key):
    middle_point = jnp.clip(0.6 * jax.random.normal(jax.random.fold_in(key, 501), (KDIM,)), -2.0, 2.0)
    gaussian = jnp.clip(jax.random.normal(jax.random.fold_in(key, 502), (REQUESTS, STEPS, KDIM)), -4.0, 4.0)
    return (middle_point, gaussian)


def decode_source(middle_point, base, mirrored):
    source = middle_point + base
    chosen = (jnp.arange(REQUESTS) < 2).astype(jnp.float32)[:, None] * mirrored
    first_step = source[:, 0] * (1.0 - chosen)
    return source.at[:, 0].set(first_step)


def draw_decode_latent(key, part):
    middle_point, gaussian = shared_parts(key)
    return decode_source(middle_point, gaussian, 0.0).astype(jnp.bfloat16)


def draw_queries(key, part):
    middle_point, gaussian = shared_parts(key)
    key = jax.random.fold_in(key, 8)
    key_scale, key_jitter = jax.random.split(key)
    strength = jnp.exp(jax.random.uniform(key_scale, (HEADS,), minval=math.log(0.15), maxval=math.log(0.3)))
    jitter = jnp.clip(jax.random.normal(key_jitter, (REQUESTS, STEPS, HEADS, KDIM)), -4.0, 4.0)
    jitter = jitter * jnp.where(jnp.arange(KDIM) < LAT, 0.3, 1.0)
    source = decode_source(middle_point, gaussian, 0.0)
    latent_part = jnp.concatenate([source[..., :LAT], jnp.zeros((REQUESTS, STEPS, ROPE), jnp.float32)], axis=-1)
    regular = latent_part[:, :, None, :] * strength[None, None, :, None] + jitter
    return regular.astype(jnp.bfloat16)


def draw_pool_pages(key, part):
    middle_point, gaussian = shared_parts(key)
    key = jax.random.fold_in(key, 9)
    key_offset, key_jitter = jax.random.split(key, 2)
    shape = (N_ROLE, GROUPS, OWNERS, PAGES_DEV, PAGE, KDIM)
    offset = 0.4 * jnp.clip(jax.random.normal(key_offset, (N_ROLE, GROUPS, OWNERS, PAGES_DEV, 1, KDIM)), -4.0, 4.0)
    jitter = 0.8 * jnp.clip(jax.random.normal(key_jitter, shape), -5.0, 5.0)
    return (middle_point + offset + jitter).astype(jnp.bfloat16)


def draw_page_dest(key, part):
    key = jax.random.fold_in(key, 41)
    popular_key, key_rank, key_shuffle = jax.random.split(key, 3)
    other_slots = (OWNERS - 1) * CAP
    hot_owner = jax.random.randint(popular_key, (GROUPS, 1, 1), 0, OWNERS)
    priority = jax.random.randint(key_rank, (GROUPS, OWNERS, other_slots), 0, 4096)
    ranking = jnp.argsort(priority * other_slots + jnp.arange(other_slots), axis=-1)
    picked = ranking[..., :PAGES_DEV - CAP]
    owner_pick = picked // CAP
    owner_real = owner_pick + (owner_pick >= hot_owner).astype(jnp.int32)
    dest_rest = owner_real * CAP + picked % CAP
    dest_hot = jnp.broadcast_to(hot_owner * CAP + jnp.arange(CAP), (GROUPS, OWNERS, CAP))
    destinations = jnp.concatenate([dest_hot, dest_rest], axis=-1)
    shuffle_keys = jax.random.randint(key_shuffle, (GROUPS, OWNERS, PAGES_DEV), 0, 4096)
    shuffle = jnp.argsort(shuffle_keys * PAGES_DEV + jnp.arange(PAGES_DEV), axis=-1)
    return jnp.take_along_axis(destinations, shuffle, axis=-1).astype(jnp.int32)


def touch_ends(entries, own_key, low, high):
    index_at = [jax.random.randint(jax.random.fold_in(own_key, axis), (), 0, length) for axis, length in enumerate(entries.shape)]
    widest = entries.shape.index(max(entries.shape))
    next_to = index_at[:widest] + [(index_at[widest] + 1) % entries.shape[widest]] + index_at[widest + 1:]
    return entries.at[tuple(index_at)].set(low).at[tuple(next_to)].set(high)


def split_up(count, total, most, slope):
    loads = [(1 << 20) // math.isqrt(rank ** slope) + 1 for rank in range(2, count + 1)]
    spare, given = total - most - (count - 1), [1] * (count - 1)
    while spare > 0:
        movable = [i for i in range(count - 1) if given[i] < most]
        mass, left = sum([loads[i] for i in movable]), spare
        for i in movable:
            extra = min(most - given[i], max(1, left * loads[i] // mass), spare)
            given[i] = given[i] + extra
            spare = spare - extra
    return np.array([most] + given)


def uneven_parts(rng, amount, total, most, skew):
    if amount == 2:
        one = jax.random.randint(rng, (), max(1, total - most), min(most, total - 1) + 1)
        return jnp.stack([one, total - one])
    lengths = jnp.asarray(split_up(amount, total, most, skew), jnp.int32)
    twos = (amount - 1) // 2
    donor, sink = lengths[1:1 + 2 * twos:2], lengths[2:2 + 2 * twos:2]
    slack = jnp.minimum(donor - 1, most - sink)
    moved = jax.random.randint(jax.random.fold_in(rng, 1), (twos,), 0, 1 << 20) % (slack + 1)
    lengths = lengths.at[1:1 + 2 * twos:2].set(donor - moved).at[2:2 + 2 * twos:2].set(sink + moved)
    return lengths[jax.random.permutation(jax.random.fold_in(rng, 2), amount)]


def setup_inputs(seed: int = 0) -> dict:
    splits = jax.random.split(jax.random.key(seed), 9)
    return {
        "pool_pages": draw_pool_pages(jax.random.fold_in(splits[8], 71), 0),
        "kv_gain": jnp.clip(1.0 + 0.15 * jax.random.normal(splits[1], (LAT,), jnp.float32), 0.25, 1.75),
        "queries": draw_queries(jax.random.fold_in(splits[8], 71), 0),
        "decode_latent": draw_decode_latent(jax.random.fold_in(splits[8], 71), 0),
        "served_request": jax.random.permutation(splits[4], REQUESTS).astype(jnp.int32),
        "resident_pages": jax.vmap(lambda own: uneven_parts(own, REQ_GRP, RES_TOTAL, RES_MOST, 2))(jax.random.split(splits[5], GROUPS)).reshape((GROUPS, REQ_GRP)).astype(jnp.int32),
        "resident_tail": touch_ends(jax.random.randint(splits[6], (GROUPS, REQ_GRP), 1, PAGE + 1), jax.random.fold_in(splits[6], 1), 1, PAGE).astype(jnp.int32),
        "page_dest": draw_page_dest(jax.random.fold_in(splits[8], 71), 0),
    }


logit_scale_factor = 192.0 ** (-0.5)
epsilon = 1e-06
lowest = -1e+30

def rotate(rope_part, positions):
    halfway = rope_part.shape[-1] // 2
    frequency = 10000.0 ** (-jnp.arange(halfway, dtype=jnp.float32) / halfway)
    angles = positions[..., None].astype(jnp.float32) * frequency
    leading = rope_part[..., :halfway]
    trailing = rope_part[..., halfway:]
    cosine = jnp.cos(angles)
    sine_part = jnp.sin(angles)
    return jnp.concatenate([leading * cosine - trailing * sine_part, trailing * cosine + leading * sine_part], axis=-1)

def finish_keys(source, kv_gain, positions):
    latent_width = kv_gain.shape[0]
    widened = source.astype(jnp.float32)
    latent = widened[..., :latent_width]
    mean_square = lax.optimization_barrier(jnp.mean(latent * latent, axis=-1, keepdims=True))
    normed = latent * lax.rsqrt(mean_square + epsilon) * kv_gain
    return jnp.concatenate([normed, rotate(widened[..., latent_width:], positions)], axis=-1).astype(jnp.bfloat16)

def query_key_product(form, left, right):
    left_kept, right_kept = lax.optimization_barrier((left, right))
    return jnp.einsum(form, left_kept.astype(jnp.float32), right_kept.astype(jnp.float32), precision=lax.Precision.HIGHEST)

def largest_block(count, limit):
    return max([trial for trial in range(1, limit + 1) if count % trial == 0])

def attend(pages, requests, valid_len, query_rows, new_keys, block_size, latent_width):
    req_count, row_count, key_width = query_rows.shape
    step_count = new_keys.shape[1]
    heads_here = row_count // step_count
    page_len = pages.shape[1]
    logit_scores = query_key_product('rtk,rqk->rtq', new_keys, query_rows) * logit_scale_factor
    step_of_row = jnp.arange(row_count) // heads_here
    visible = (jnp.arange(step_count)[:, None] <= step_of_row[None, :])[None]
    logit_scores = jnp.where(visible, logit_scores, lowest)
    running_max = lax.optimization_barrier(jnp.max(logit_scores, axis=1))
    unnormed = jnp.where(visible, jnp.exp(logit_scores - running_max[:, None, :]), 0.0)
    running_sum = lax.optimization_barrier(jnp.sum(unnormed, axis=1))
    running_out = query_key_product('rtq,rtc->rqc', unnormed.astype(jnp.bfloat16), new_keys[..., :latent_width])
    block_count = pages.shape[0] // block_size
    stacked = (pages.reshape(block_count, block_size, page_len, key_width), requests.reshape(block_count, block_size), valid_len.reshape(block_count, block_size))

    def page_step(state_in, block_data):
        running_out, running_sum, running_max = state_in
        block_of_keys, block_req, block_len = block_data
        local_queries = query_rows[block_req]
        logit_scores = query_key_product('zdi,zli->zdl', block_of_keys, local_queries) * logit_scale_factor
        visible = (jnp.arange(page_len)[None, :] < block_len[:, None])[:, :, None]
        logit_scores = jnp.where(visible, logit_scores, lowest)
        page_max = lax.optimization_barrier(jnp.max(logit_scores, axis=1))
        unnormed = jnp.where(visible, jnp.exp(logit_scores - page_max[:, None, :]), 0.0)
        page_sum = lax.optimization_barrier(jnp.sum(unnormed, axis=1))
        page_out = query_key_product('btq,btc->bqc', unnormed.astype(jnp.bfloat16), block_of_keys[..., :latent_width])
        member = block_req[None, :] == jnp.arange(req_count)[:, None]
        block_max = lax.optimization_barrier(jnp.max(jnp.where(member[:, :, None], page_max[None], lowest), axis=1))
        new_max = jnp.maximum(running_max, block_max)
        carry_over = jnp.exp(running_max - new_max)
        factor = jnp.exp(page_max - new_max[block_req])
        running_out = (running_out * carry_over[..., None]).at[block_req].add(page_out * factor[..., None])
        running_sum = (running_sum * carry_over).at[block_req].add(page_sum * factor)
        return ((running_out, running_sum, new_max), None)
    (running_out, running_sum, running_max), _ = lax.scan(page_step, (running_out, running_sum, running_max), stacked)
    return (running_out, running_sum)

def reference(pool_pages, kv_gain, queries, decode_latent, served_request, resident_pages, resident_tail, page_dest):
    attention_parts = []
    cache_parts = []
    owner_ids = jnp.arange(OWNERS, dtype=jnp.int32)
    page_ids = jnp.arange(PAGES_DEV, dtype=jnp.int32)
    prompt_page = page_ids // SPAN_PAGES
    for group_index in range(GROUPS):
        counts = resident_pages[group_index]
        tail_len = resident_tail[group_index]
        res_len = PAGE * (counts - 1) + tail_len
        positions = res_len[prompt_page][None, :, None] + ((owner_ids[:, None] * SPAN_PAGES + page_ids[None, :] % SPAN_PAGES) * PAGE)[:, :, None] + jnp.arange(PAGE, dtype=jnp.int32)[None, None, :]
        fresh_keys = finish_keys(pool_pages[0, group_index], kv_gain, positions)
        destinations = page_dest[group_index]
        owner_of = destinations // CAP
        slot_of = owner_ids[:, None] * CAP + destinations % CAP
        received = jnp.zeros((OWNERS, OWNERS * CAP, PAGE, KDIM), jnp.bfloat16).at[owner_of, slot_of].set(fresh_keys)
        cache_parts.append(received)
        run_ends = jnp.cumsum(counts).astype(jnp.int32)
        starts = run_ends - counts
        flat_index = (page_ids[None, :] * OWNERS + owner_ids[:, None]).reshape(-1)
        res_req = lax.optimization_barrier(jnp.sum((flat_index[:, None] >= run_ends[None, :]).astype(jnp.int32), axis=1)).astype(jnp.int32)
        res_page = flat_index - starts[res_req]
        res_valid = jnp.where(res_page < counts[res_req] - 1, PAGE, tail_len[res_req]).astype(jnp.int32)
        pages = jnp.concatenate([fresh_keys.reshape(-1, PAGE, KDIM), pool_pages[1, group_index].reshape(-1, PAGE, KDIM)], axis=0)
        requests = jnp.concatenate([jnp.tile(prompt_page, OWNERS), res_req]).astype(jnp.int32)
        valid_len = jnp.concatenate([jnp.full((OWNERS * PAGES_DEV,), PAGE, jnp.int32), res_valid]).astype(jnp.int32)
        arrivals = served_request[group_index * REQ_GRP:(group_index + 1) * REQ_GRP]
        query_rows = queries[arrivals].reshape(REQ_GRP, STEPS * HEADS, KDIM)
        new_keys = finish_keys(decode_latent[arrivals], kv_gain, res_len[:, None] + SPAN + jnp.arange(STEPS, dtype=jnp.int32)[None, :])
        block_size = largest_block(pages.shape[0], 16)
        running_out, running_sum = attend(pages, requests, valid_len, query_rows, new_keys, block_size, LAT)
        result = (running_out / running_sum[..., None]).astype(jnp.bfloat16)
        attention_parts.append(result.reshape(REQ_GRP, STEPS, HEADS, LAT))
    return (jnp.concatenate(attention_parts, axis=0), jnp.stack(cache_parts, axis=0))
```

```python
import functools

import jax
import jax.numpy as jnp
from jax import lax
from jax.experimental import pallas as pl
from jax.experimental.pallas import tpu as pltpu
from jax.sharding import PartitionSpec as P

logit_scale_factor = 192.0 ** (-0.5)
epsilon = 1e-06
lowest = -1e30

VMEM_LIMIT = 48 * 1024 * 1024
LAT = 512
KDIM = 576
PAGE = 64
OWNERS = 32
RING_Y = 4
RING_Z = 8


def rotate(rope_part, positions):
    halfway = rope_part.shape[-1] // 2
    frequency = 10000.0 ** (-jnp.arange(halfway, dtype=jnp.float32) / halfway)
    angles = positions[..., None].astype(jnp.float32) * frequency
    leading = rope_part[..., :halfway]
    trailing = rope_part[..., halfway:]
    cosine = jnp.cos(angles)
    sine_part = jnp.sin(angles)
    return jnp.concatenate(
        [leading * cosine - trailing * sine_part, trailing * cosine + leading * sine_part], axis=-1
    )


def finish_keys(source, kv_gain, positions):
    widened = source.astype(jnp.float32)
    latent = widened[..., :LAT]
    mean_square = jnp.mean(latent * latent, axis=-1, keepdims=True)
    normed = latent * lax.rsqrt(mean_square + epsilon) * kv_gain
    return jnp.concatenate([normed, rotate(widened[..., LAT:], positions)], axis=-1).astype(
        jnp.bfloat16
    )


def rope_table(positions):
    frequency = 10000.0 ** (-jnp.arange(32, dtype=jnp.float32) / 32)
    angles = positions[..., None].astype(jnp.float32) * frequency
    cosine = jnp.cos(angles)
    sine_part = jnp.sin(angles)
    return jnp.concatenate([cosine, cosine, -sine_part, sine_part], axis=-1)


def finish_kernel(
    inverse_ref, role_ref, own_ref, partner_ref, gain_ref, table_ref, fresh_ref, resident_ref, out_ref
):
    at_prefill = role_ref[0] == 0
    gain = gain_ref[...]

    def one_page(i, _):
        mine = own_ref[i]
        other = partner_ref[i]
        raw = jnp.where(at_prefill, mine, other).astype(jnp.float32)
        resident_ref[i] = jnp.where(at_prefill, other, mine)
        latent = raw[:, :LAT]
        mean_square = jnp.sum(latent * latent, axis=-1, keepdims=True) * (1.0 / LAT)
        normed = latent * lax.rsqrt(mean_square + epsilon) * gain
        rope = raw[:, LAT:]
        swapped = jnp.concatenate([rope[:, 32:], rope[:, :32]], axis=-1)
        table = table_ref[i]
        turned = rope * table[:, :64] + swapped * table[:, 64:]
        fresh_ref[i] = jnp.concatenate([normed, turned], axis=-1).astype(jnp.bfloat16)
        return 0

    lax.fori_loop(0, own_ref.shape[0], one_page, 0)

    def one_slot(t, _):
        page = inverse_ref[t]
        found = fresh_ref[jnp.maximum(page, 0)]
        out_ref[t] = jnp.where(page >= 0, found, jnp.zeros_like(found))
        return 0

    lax.fori_loop(0, OWNERS, one_slot, 0)


def finish_and_pack(inverse, role, own, partner, gain, table):
    pages = own.shape[0]
    smem = pl.BlockSpec(memory_space=pltpu.SMEM)
    vmem = pl.BlockSpec(memory_space=pltpu.VMEM)
    page = jax.ShapeDtypeStruct((pages, PAGE, KDIM), jnp.bfloat16)
    return pl.pallas_call(
        finish_kernel,
        out_shape=(page, page, jax.ShapeDtypeStruct((OWNERS, PAGE, KDIM), jnp.bfloat16)),
        in_specs=[smem, smem, vmem, vmem, vmem, vmem],
        out_specs=(vmem, vmem, vmem),
        compiler_params=pltpu.CompilerParams(vmem_limit_bytes=VMEM_LIMIT),
        cost_estimate=pl.CostEstimate(flops=20_000_000, bytes_accessed=10_000_000, transcendentals=0),
        name="finish_and_pack",
    )(inverse, role, own, partner, gain.reshape(1, LAT), table)


def attend_kernel(
    begin_ref, end_ref, valid_ref, owner_ref,
    q_ref, fresh_ref, resident_ref, newk_ref,
    o_ref, ml_ref,
    acc, m_ref, l_ref,
):
    pair = pl.program_id(0)
    rows = acc.shape[0]

    @pl.when(pair == 0)
    def _():
        ml_ref[...] = jnp.zeros(ml_ref.shape, jnp.float32)

    lane = lax.broadcasted_iota(jnp.int32, (rows, 2 * PAGE), 1)
    low = lane < PAGE
    step_of_row = (lax.broadcasted_iota(jnp.int32, (rows, 2 * PAGE), 0) % 8) // 2

    def weigh(q, keys, visible, m_before):
        s = lax.dot_general(q, keys, (((1,), (1,)), ((), ())), preferred_element_type=jnp.float32)
        s = s * logit_scale_factor
        if visible is not None:
            s = jnp.where(visible, s, lowest)
        m1 = jnp.max(jnp.where(low, s, lowest), axis=1, keepdims=True)
        m2 = jnp.max(jnp.where(low, lowest, s), axis=1, keepdims=True)
        mb = jnp.where(low, m1, m2)
        e = jnp.exp(s - mb)
        if visible is not None:
            e = jnp.where(visible, e, 0.0)
        m_now = jnp.maximum(m1, m2)
        if m_before is not None:
            m_now = jnp.maximum(m_now, m_before)
        f = jnp.where(low, jnp.exp(m1 - m_now), jnp.exp(m2 - m_now))
        l = jnp.sum(e * f, axis=1, keepdims=True)
        wide = e.astype(jnp.bfloat16).astype(jnp.float32) * f
        hi = wide.astype(jnp.bfloat16)
        lo = (wide - hi.astype(jnp.float32)).astype(jnp.bfloat16)
        values = keys[:, :LAT]
        o = jnp.dot(
            jnp.concatenate([hi, lo], axis=1),
            jnp.concatenate([values, values], axis=0),
            preferred_element_type=jnp.float32,
        )
        return m_now, l, o

    def update(q, keys, visible):
        before = m_ref[...]
        m_now, l, o = weigh(q, keys, visible, before)
        carry = jnp.exp(before - m_now)
        m_ref[...] = m_now
        l_ref[...] = l_ref[...] * carry + l
        acc[...] = acc[...] * carry + o

    for jj in range(2):
        j = pair * 2 + jj
        blocks = [
            q_ref[z * RING_Y + y].astype(jnp.float32)[jj * 8 : jj * 8 + 8]
            for y in range(RING_Y)
            for z in range(RING_Z)
        ]
        q = jnp.concatenate(blocks, axis=0).astype(jnp.bfloat16)
        keys = fresh_ref[2 * jj : 2 * jj + 2].reshape(2 * PAGE, KDIM)
        m_now, l, o = weigh(q, keys, None, None)
        m_ref[...] = m_now
        l_ref[...] = l
        acc[...] = o
        begin = begin_ref[j]
        end = end_ref[j]

        def two_pages(i, _):
            first = begin + 2 * i
            second = jnp.minimum(first + 1, end - 1)
            keys = jnp.concatenate([resident_ref[first], resident_ref[second]], axis=0)
            live_first = valid_ref[first]
            live_second = jnp.where(first + 1 < end, valid_ref[second], 0)
            visible = lane < jnp.where(low, live_first, PAGE + live_second)
            update(q, keys, visible)
            return 0

        lax.fori_loop(0, (end - begin + 1) // 2, two_pages, 0)

        @pl.when(j == owner_ref[0])
        def _():
            visible = lane <= jnp.where(lane < 4, step_of_row, -1)
            update(q, newk_ref[...], visible)

        codes, scale = encode(acc[...])
        o_ref[:, jj] = codes.reshape(RING_Y, rows // RING_Y, LAT)
        stats = jnp.where(lane == 16 + j, l_ref[...], jnp.where(lane == 32 + j, scale, ml_ref[...]))
        ml_ref[...] = jnp.where(lane == j, m_ref[...], stats)


def attend(begin, end, valid, owner, q_all, fresh, resident, newk):
    rows = 8 * OWNERS
    smem = pl.BlockSpec(memory_space=pltpu.SMEM)
    pairs = 6
    return pl.pallas_call(
        attend_kernel,
        grid=(pairs,),
        out_shape=(
            jax.ShapeDtypeStruct((RING_Y, 2 * pairs, rows // RING_Y, LAT), jnp.int16),
            jax.ShapeDtypeStruct((rows, 128), jnp.float32),
        ),
        in_specs=[
            smem, smem, smem, smem,
            pl.BlockSpec((OWNERS, 16, KDIM), lambda p: (0, p, 0)),
            pl.BlockSpec((4, PAGE, KDIM), lambda p: (p, 0, 0)),
            pl.BlockSpec((24, PAGE, KDIM), lambda p: (0, 0, 0)),
            pl.BlockSpec((2 * PAGE, KDIM), lambda p: (0, 0)),
        ],
        out_specs=(
            pl.BlockSpec((RING_Y, 2, rows // RING_Y, LAT), lambda p: (0, p, 0, 0)),
            pl.BlockSpec((rows, 128), lambda p: (0, 0)),
        ),
        scratch_shapes=[
            pltpu.VMEM((rows, LAT), jnp.float32),
            pltpu.VMEM((rows, 1), jnp.float32),
            pltpu.VMEM((rows, 1), jnp.float32),
        ],
        compiler_params=pltpu.CompilerParams(vmem_limit_bytes=VMEM_LIMIT),
        cost_estimate=pl.CostEstimate(
            flops=2_000_000_000, bytes_accessed=11_000_000, transcendentals=2_000_000
        ),
        name="attend_pages",
    )(begin, end, valid, owner, q_all, fresh, resident, newk)


MESH_IDS = pl.DeviceIdType.MESH
CODE_TOP = 32767.0
CHUNKS = 2
HALF = 6 // CHUNKS


def greet(devices):
    barrier = pltpu.get_barrier_semaphore()
    for device in devices:
        pl.semaphore_signal(barrier, inc=1, device_id=device, device_id_type=MESH_IDS)
    pl.semaphore_wait(barrier, len(devices))


def merge_stats(blocks):
    lane = lax.broadcasted_iota(jnp.int32, blocks[0].shape, 1)
    top = functools.reduce(jnp.maximum, blocks)
    total = jnp.zeros_like(top)
    weights = []
    for block in blocks:
        part = jnp.exp(jnp.where(lane < 16, block - top, 0.0))
        total = total + part * pltpu.roll(block, 112, 1)
        weights.append(part * pltpu.roll(block, 96, 1))
    return top, total, weights


def column(block, index):
    lane = lax.broadcasted_iota(jnp.int32, block.shape, 1)
    return jnp.sum(jnp.where(lane == index, block, 0.0), axis=1, keepdims=True)


def encode(values):
    scale = jnp.max(jnp.abs(values), axis=1, keepdims=True)
    codes = jnp.floor(values * (CODE_TOP / jnp.maximum(scale, 1e-30)) + 0.5)
    return codes.astype(jnp.int32).astype(jnp.int16), scale * (1.0 / CODE_TOP)


def decode(codes):
    return codes.astype(jnp.int32).astype(jnp.float32)


def join_stats(top, total, scales):
    lane = lax.broadcasted_iota(jnp.int32, top.shape, 1)
    return jnp.where(lane < 16, top, jnp.where(lane < 32, pltpu.roll(total, 16, 1), scales))


def merge_kernel(
    o_ref, ml_ref, out_ref,
    relay_in, direct_in, merged, merged_in, stat_in, mstat, mstat_in,
    zcodes, zin, zstat, zstat_in, values,
    send_y, recv_y, send_z, recv_z,
):
    role = lax.axis_index("role")
    group = lax.axis_index("grp")
    me = lax.axis_index("dev")
    z = me // RING_Y
    y = me % RING_Y

    def at(zz, yy):
        return (role, group, zz * RING_Y + yy)

    up = (y + 1) % RING_Y
    down = (y + 3) % RING_Y
    far = (y + 2) % RING_Y
    greet([at(z, up), at(z, down)] + [at((z + k) % RING_Z, y) for k in range(1, RING_Z)])
    copies = []

    def push(src, dst, sends, recvs, index, target):
        copy = pltpu.make_async_remote_copy(
            src_ref=src, dst_ref=dst, send_sem=sends.at[index], recv_sem=recvs.at[index],
            device_id=target, device_id_type=MESH_IDS,
        )
        copy.start()
        copies.append(copy)
        return copy

    ways = ((up, down), (down, up))
    stat_far, stat_near, relayed, direct = {}, {}, {}, {}
    for way, (ahead, _) in enumerate(ways):
        stat_far[way] = push(ml_ref.at[far], stat_in.at[2 * way], send_y, recv_y, 2 * way, at(z, ahead))
        stat_near[way] = push(
            ml_ref.at[ahead], stat_in.at[2 * way + 1], send_y, recv_y, 2 * way + 1, at(z, ahead)
        )
    for c in range(CHUNKS):
        for way, (ahead, _) in enumerate(ways):
            base = 6 * way + HALF * c
            relayed[c, way] = push(
                o_ref.at[far, pl.ds(base, HALF)], relay_in.at[way, c], send_y, recv_y,
                4 + 2 * c + way, at(z, ahead),
            )
        for way, (ahead, _) in enumerate(ways):
            base = 6 * (1 - way) + HALF * c
            direct[c, way] = push(
                o_ref.at[ahead, pl.ds(base, HALF)], direct_in.at[way, c], send_y, recv_y,
                4 + 2 * CHUNKS + 2 * c + way, at(z, ahead),
            )

    passed, passed_stat = {}, {}
    for c in range(CHUNKS):
        for way, (ahead, _) in enumerate(ways):
            if c == 0:
                stat_far[way].wait_recv()
            relayed[c, way].wait_recv()
            top, total, weights = merge_stats([stat_in[2 * way], ml_ref[ahead]])
            base = 6 * way + HALF * c

            def relay_one(i, scales, way=way, c=c, base=base, ahead=ahead, weights=weights):
                mixed = decode(relay_in[way, c, i]) * column(weights[0], base + i)
                mixed = mixed + decode(o_ref[ahead, base + i]) * column(weights[1], base + i)
                codes, scale = encode(mixed)
                merged[way, c, i] = codes
                lane = lax.broadcasted_iota(jnp.int32, scales.shape, 1)
                return jnp.where(lane == 32 + base + i, scale, scales)

            scales = lax.fori_loop(0, HALF, relay_one, jnp.zeros_like(top))
            mstat[way, c] = join_stats(top, total, scales)
            first = 4 + 4 * CHUNKS + 4 * c + 2 * way
            passed[c, way] = push(
                merged.at[way, c], merged_in.at[way, c], send_y, recv_y, first, at(z, ahead)
            )
            passed_stat[c, way] = push(
                mstat.at[way, c], mstat_in.at[way, c], send_y, recv_y, first + 1, at(z, ahead)
            )

    arrivals = {}
    for c in range(CHUNKS):
        if c == 0:
            for way in range(2):
                stat_near[way].wait_recv()
        stats = []
        for way in range(2):
            passed_stat[c, way].wait_recv()
            passed[c, way].wait_recv()
            direct[c, 1 - way].wait_recv()
            stats.append(merge_stats([ml_ref[y], mstat_in[way, c], stat_in[2 * (1 - way) + 1]]))
        lane = lax.broadcasted_iota(jnp.int32, ml_ref[y].shape, 1)
        scales = jnp.zeros(ml_ref[y].shape, jnp.float32)
        for way in range(2):
            base = 6 * way + HALF * c
            top, total, weights = stats[way]

            def land_one(i, scales, way=way, c=c, base=base, weights=weights):
                mixed = decode(o_ref[y, base + i]) * column(weights[0], base + i)
                mixed = mixed + decode(merged_in[way, c, i]) * column(weights[1], base + i)
                mixed = mixed + decode(direct_in[1 - way, c, i]) * column(weights[2], base + i)
                scale = jnp.maximum(jnp.max(jnp.abs(mixed), axis=1, keepdims=True), 1e-30)
                values[way * HALF + i] = jnp.floor(mixed * (CODE_TOP / scale) + 0.5)
                return jnp.where(lane == 32 + base + i, scale * (1.0 / CODE_TOP), scales)

            scales = lax.fori_loop(0, HALF, land_one, scales)
        use_up = (lane % 16) < 6
        top = jnp.where(use_up, stats[0][0], stats[1][0])
        total = jnp.where(use_up, stats[0][1], stats[1][1])
        zstat[c] = join_stats(top, total, scales)

        def split_one(zz, _, c=c):
            rows = values[:, pl.ds(pl.multiple_of(zz * 8, 8), 8), :]
            rows = rows.reshape(2 * HALF * 8, LAT)
            zcodes[c, zz] = rows.astype(jnp.int32).astype(jnp.int16)
            return 0

        lax.fori_loop(0, RING_Z, split_one, 0)
        for k in (4, 3, 5, 2, 6, 1, 7):
            there = (z + k) % RING_Z
            back = RING_Z - k
            index = 2 * (c * RING_Z + k)
            arrivals[c, k] = (
                push(
                    zstat.at[c, pl.ds(there * 8, 8)], zstat_in.at[c, k], send_z, recv_z, index + 1,
                    at(there, y),
                ),
                push(zcodes.at[c, there], zin.at[c, k], send_z, recv_z, index, at(there, y)),
            )

    for c in range(CHUNKS):
        for k in range(1, RING_Z):
            for copy in arrivals[c, k]:
                copy.wait_recv()
        blocks = [zstat[c, pl.ds(pl.multiple_of(z * 8, 8), 8), :]]
        blocks = blocks + [zstat_in[c, k] for k in range(1, RING_Z)]
        top, total, weights = merge_stats(blocks)
        for way in range(2):
            sums = []
            for i in range(HALF):
                j = 6 * way + HALF * c + i
                sums.append(1.0 / column(total, j))
            mixed = None
            for k in range(RING_Z):
                codes = zcodes.at[c, z] if k == 0 else zin.at[c, k]
                part = decode(codes[...])[way * HALF * 8 : (way + 1) * HALF * 8]
                factor = jnp.concatenate(
                    [column(weights[k], 6 * way + HALF * c + i) * sums[i] for i in range(HALF)], axis=0
                )
                mixed = part * factor if mixed is None else mixed + part * factor
            first = (6 * way + HALF * c) * 8
            out_ref[first : first + HALF * 8, :] = mixed
    for copy in copies:
        copy.wait_send()


def merge_over_owners(o_codes, ml):
    half = (2, CHUNKS, HALF, 64, LAT)
    vmem = pl.BlockSpec(memory_space=pltpu.VMEM)
    return pl.pallas_call(
        merge_kernel,
        out_shape=jax.ShapeDtypeStruct((96, LAT), jnp.float32),
        in_specs=[vmem, vmem],
        out_specs=vmem,
        scratch_shapes=[
            pltpu.VMEM(half, jnp.int16),
            pltpu.VMEM(half, jnp.int16),
            pltpu.VMEM(half, jnp.int16),
            pltpu.VMEM(half, jnp.int16),
            pltpu.VMEM((4, 64, 128), jnp.float32),
            pltpu.VMEM((2, CHUNKS, 64, 128), jnp.float32),
            pltpu.VMEM((2, CHUNKS, 64, 128), jnp.float32),
            pltpu.VMEM((CHUNKS, RING_Z, 16 * HALF, LAT), jnp.int16),
            pltpu.VMEM((CHUNKS, RING_Z, 16 * HALF, LAT), jnp.int16),
            pltpu.VMEM((CHUNKS, 64, 128), jnp.float32),
            pltpu.VMEM((CHUNKS, RING_Z, 8, 128), jnp.float32),
            pltpu.VMEM((2 * HALF, 64, LAT), jnp.float32),
            pltpu.SemaphoreType.DMA((4 + 8 * CHUNKS,)),
            pltpu.SemaphoreType.DMA((4 + 8 * CHUNKS,)),
            pltpu.SemaphoreType.DMA((2 * CHUNKS * RING_Z,)),
            pltpu.SemaphoreType.DMA((2 * CHUNKS * RING_Z,)),
        ],
        compiler_params=pltpu.CompilerParams(
            vmem_limit_bytes=VMEM_LIMIT, collective_id=1, has_side_effects=True
        ),
        cost_estimate=pl.CostEstimate(
            flops=20_000_000, bytes_accessed=100_000_000, transcendentals=0
        ),
        name="merge_over_owners",
    )(o_codes, ml)


def gather_kernel(
    served_ref, q_ref, lat_ref, out_ref, lat_out_ref,
    xbuf, lbuf, chosen,
    send_x, recv_x, send_sem, recv_sem, local_sem,
):
    role = lax.axis_index("role")
    group = lax.axis_index("grp")
    me = lax.axis_index("dev")
    z = me // RING_Y
    y = me % RING_Y

    def at(zz, yy):
        return (role, group, zz * RING_Y + yy)

    neighbours = {
        "up": at(z, (y + 1) % RING_Y),
        "down": at(z, (y + 3) % RING_Y),
        "in": at((z + 1) % RING_Z, y),
        "out": at((z + 7) % RING_Z, y),
    }
    greet(list(neighbours.values()) + [(role, (group + k) % 4, me) for k in range(1, 4)])
    copies = []
    arriving = []
    for k in (2, 1, 3):
        target = (role, (group + k) % 4, me)
        for src, buf, index in ((q_ref, xbuf, 2 * k), (lat_ref, lbuf, 2 * k + 1)):
            copy = pltpu.make_async_remote_copy(
                src_ref=src, dst_ref=buf.at[group], send_sem=send_x.at[index],
                recv_sem=recv_x.at[index], device_id=target, device_id_type=MESH_IDS,
            )
            copy.start()
            copies.append(copy)
            arriving.append(copy)
    xbuf[group] = q_ref[...]
    lbuf[group] = lat_ref[...]
    for copy in arriving:
        copy.wait_recv()

    def pick(index):
        pair = xbuf[index // 12, (index % 12) // 2].astype(jnp.float32)
        return jnp.where(index % 2 == 0, pair[:8], pair[8:])

    for p in range(6):
        both = jnp.concatenate([pick(served_ref[2 * p]), pick(served_ref[2 * p + 1])], axis=0)
        chosen[16 * p : 16 * p + 16, :] = both.astype(jnp.bfloat16)
    mine = served_ref[jnp.minimum(me, 11)]
    lat_out_ref[...] = lbuf[mine // 12, (mine % 12) // 4]

    def slot(dz, dy):
        return ((z - dz + 2 * RING_Z) % RING_Z) * RING_Y + (y - dy + 2 * RING_Y) % RING_Y

    local = pltpu.make_async_copy(chosen, out_ref.at[me], local_sem)
    local.start()
    waits = {}

    def send(half, dz, dy, to):
        rows = pl.ds(48 * half, 48)
        place = slot(dz, dy)
        source = chosen.at[rows] if (dz, dy) == (0, 0) else out_ref.at[place, rows]
        ndz, ndy = dz, dy
        if to == "in":
            ndz = dz + 1
        if to == "out":
            ndz = dz - 1
        if to == "up":
            ndy = dy + 1
        if to == "down":
            ndy = dy - 1
        index = half * 32 + (ndz % RING_Z) * RING_Y + ndy % RING_Y
        copy = pltpu.make_async_remote_copy(
            src_ref=source, dst_ref=out_ref.at[place, rows], send_sem=send_sem.at[index],
            recv_sem=recv_sem.at[index], device_id=neighbours[to], device_id_type=MESH_IDS,
        )
        copy.start()
        copies.append(copy)
        here = out_ref.at[slot(ndz, ndy), rows]
        waits[half, ndz, ndy] = pltpu.make_async_remote_copy(
            src_ref=here, dst_ref=here, send_sem=send_sem.at[index],
            recv_sem=recv_sem.at[index], device_id=neighbours[to], device_id_type=MESH_IDS,
        )
        return (half, ndz, ndy)

    def z_steps(half, dz, dy):
        deep = 4 if (half == 0 or dy in (0, 1)) else 3
        steps = []
        if 0 <= dz < deep:
            steps.append("in")
        if 0 >= dz > deep - 7:
            steps.append("out")
        return steps

    def y_steps(half, dz, dy):
        if dy == 0:
            return ["up", "down"]
        if dy == 1 and (half == 1 or dz % 2 == 0):
            return ["up"]
        if dy == -1 and half == 0 and dz % 2 == 1:
            return ["down"]
        return []

    def forward(block):
        half, dz, dy = block
        steps = []
        if half == 0:
            steps = (z_steps(half, dz, dy) if dy == 0 else []) + y_steps(half, dz, dy)
        else:
            steps = (y_steps(half, dz, dy) if dz == 0 else []) + z_steps(half, dz, dy)
        return [send(half, dz, dy, to) for to in steps]

    frontier = forward((0, 0, 0)) + forward((1, 0, 0))
    while frontier:
        later = []
        for block in frontier:
            waits[block].wait_recv()
            later = later + forward(block)
        frontier = later
    local.wait()
    for copy in copies:
        copy.wait_send()


def gather_queries(served, queries, latents):
    vmem = pl.BlockSpec(memory_space=pltpu.VMEM)
    return pl.pallas_call(
        gather_kernel,
        out_shape=(
            jax.ShapeDtypeStruct((OWNERS, 96, KDIM), jnp.bfloat16),
            jax.ShapeDtypeStruct((16, KDIM), jnp.bfloat16),
        ),
        in_specs=[pl.BlockSpec(memory_space=pltpu.SMEM), vmem, vmem],
        out_specs=(pl.BlockSpec(memory_space=pl.ANY), vmem),
        scratch_shapes=[
            pltpu.VMEM((4, 6, 16, KDIM), jnp.bfloat16),
            pltpu.VMEM((4, 3, 16, KDIM), jnp.bfloat16),
            pltpu.VMEM((96, KDIM), jnp.bfloat16),
            pltpu.SemaphoreType.DMA((8,)),
            pltpu.SemaphoreType.DMA((8,)),
            pltpu.SemaphoreType.DMA((64,)),
            pltpu.SemaphoreType.DMA((64,)),
            pltpu.SemaphoreType.DMA,
        ],
        compiler_params=pltpu.CompilerParams(
            vmem_limit_bytes=VMEM_LIMIT, collective_id=2, has_side_effects=True
        ),
        cost_estimate=pl.CostEstimate(
            flops=1_000_000, bytes_accessed=80_000_000, transcendentals=0
        ),
        name="gather_queries",
    )(served, queries, latents)


def per_device(
    pool_pages,
    kv_gain,
    queries,
    decode_latent,
    served_request,
    resident_pages,
    resident_tail,
    page_dest,
):
    role = lax.axis_index("role")
    group = lax.axis_index("grp")
    owner = lax.axis_index("dev")
    at_prefill = role == 0
    own = pool_pages[0, 0, 0]
    pages_dev = own.shape[0]
    swap = [(0, 1), (1, 0)]
    partner = lax.ppermute(own, "role", swap)

    counts = resident_pages[0]
    tail_len = resident_tail[0]
    req_grp = counts.shape[0]
    per_prompt = pages_dev // req_grp
    res_len = PAGE * (counts - 1) + tail_len
    page_ids = jnp.arange(pages_dev, dtype=jnp.int32)
    positions = (
        res_len[page_ids // per_prompt][:, None]
        + ((owner * per_prompt + page_ids % per_prompt) * PAGE)[:, None]
        + jnp.arange(PAGE, dtype=jnp.int32)[None, :]
    )
    targets = lax.dynamic_index_in_dim(page_dest[0], owner, 0, keepdims=False)
    wanted = jnp.arange(OWNERS, dtype=jnp.int32) * 2 + role
    hits = targets[None, :] == wanted[:, None]
    inverse = jnp.max(jnp.where(hits, page_ids[None, :], -1), axis=1).astype(jnp.int32)
    role_arr = role.astype(jnp.int32).reshape(1)
    fresh, resident, outgoing = finish_and_pack(
        inverse, role_arr, own, partner, kv_gain, rope_table(positions)
    )
    routed = lax.all_to_all(outgoing, "dev", split_axis=0, concat_axis=0, tiled=True)
    routed_other = lax.ppermute(routed, "role", swap)
    received = jnp.stack(
        [jnp.where(at_prefill, routed, routed_other), jnp.where(at_prefill, routed_other, routed)],
        axis=1,
    ).reshape(2 * OWNERS, PAGE, KDIM)

    run_ends = jnp.cumsum(counts)
    starts = run_ends - counts
    flat = page_ids * OWNERS + owner
    begin = jnp.sum((flat[None, :] < starts[:, None]).astype(jnp.int32), axis=1)
    end = jnp.sum((flat[None, :] < run_ends[:, None]).astype(jnp.int32), axis=1)
    res_req = jnp.sum((flat[:, None] >= run_ends[None, :]).astype(jnp.int32), axis=1)
    valid = jnp.where(flat - starts[res_req] < counts[res_req] - 1, PAGE, tail_len[res_req])

    heads_here = queries.shape[2]
    steps = queries.shape[1]
    rows_here = steps * heads_here
    serving = lax.dynamic_slice_in_dim(served_request, group * req_grp, req_grp)
    q_all, latents = gather_queries(
        serving, queries.reshape(6, 16, KDIM), decode_latent.reshape(3, 16, KDIM)
    )
    mine = jnp.minimum(owner, req_grp - 1)
    own_latent = lax.dynamic_slice_in_dim(latents, (serving[mine] % 4) * steps, steps)
    new_positions = res_len[mine] + per_prompt * PAGE * OWNERS + jnp.arange(steps, dtype=jnp.int32)
    newk = finish_keys(own_latent, kv_gain, new_positions)
    newk = jnp.pad(newk, ((0, 2 * PAGE - steps), (0, 0)))

    o_part, ml = attend(
        begin, end, valid.astype(jnp.int32), owner.astype(jnp.int32).reshape(1),
        q_all, fresh, resident, newk,
    )
    merged = merge_over_owners(o_part, ml.reshape(RING_Y, 2 * OWNERS, 128))
    attention = merged.astype(jnp.bfloat16)
    attention = attention.reshape(req_grp, steps, heads_here, LAT)
    return (attention, received[None, None])


def solution(mesh):
    in_specs = (
        P("role", "grp", "dev", None, None, None),
        P(),
        P("grp", None, ("role", "dev"), None),
        P("grp", None, None),
        P(),
        P("grp", None),
        P("grp", None),
        P("grp", None, None),
    )
    out_specs = (P("grp", None, ("role", "dev"), None), P("grp", "dev", None, None, None))
    return jax.shard_map(
        per_device, mesh=mesh, in_specs=in_specs, out_specs=out_specs, check_vma=False
    )
```

```python
import functools

import jax
import jax.numpy as jnp
from jax import lax
from jax.experimental import pallas as pl
from jax.experimental.pallas import tpu as pltpu
from jax.sharding import PartitionSpec as P

logit_scale_factor = 192.0 ** (-0.5)
epsilon = 1e-06
lowest = -1e30

VMEM_LIMIT = 58 * 1024 * 1024
LAT = 512
KDIM = 576
PAGE = 64
OWNERS = 32
RING_Y = 4
RING_Z = 8


SERVED, BEGIN, END, REQUEST, VALID, SAME, INVERSE = 0, 12, 24, 36, 60, 84, 108


def rope_table(positions):
    lane = jnp.arange(128)
    frequency = 10000.0 ** (-(lane % 32).astype(jnp.float32) / 32)
    angles = positions[..., None].astype(jnp.float32) * frequency
    sine_part = jnp.sin(angles)
    turned = jnp.where(lane < 96, -sine_part, sine_part)
    return jnp.where(lane < 64, jnp.cos(angles), turned)


MESH_IDS = pl.DeviceIdType.MESH
CODE_TOP = 32767.0
CHUNKS = 2
HALF = 6 // CHUNKS


DISTANCES = [(0, dy) for dy in (2, 1, 3)]
DISTANCES = DISTANCES + [(dz, dy) for dy in (1, 3, 2, 0) for dz in (4, 3, 5, 2, 6, 1, 7)]
DISTANCES = DISTANCES + [(0, 0)]
EARLY, BEFORE_ATTENTION = 6, 20


def everyone(role, group, z, y):
    return [
        (role, group, ((z + dz) % RING_Z) * RING_Y + (y + dy) % RING_Y)
        for dz, dy in DISTANCES
        if (dz, dy) != (0, 0)
    ]


def greet(devices):
    barrier = pltpu.get_barrier_semaphore()
    for device in devices:
        pl.semaphore_signal(barrier, inc=1, device_id=device, device_id_type=MESH_IDS)
    pl.semaphore_wait(barrier, len(devices))


def merge_stats(blocks):
    lane = lax.broadcasted_iota(jnp.int32, blocks[0].shape, 1)
    top = functools.reduce(jnp.maximum, blocks)
    total = jnp.zeros_like(top)
    weights = []
    for block in blocks:
        part = jnp.exp(jnp.where(lane < 16, block - top, 0.0))
        total = total + part * pltpu.roll(block, 112, 1)
        weights.append(part * pltpu.roll(block, 96, 1))
    return top, total, weights


def column(block, index):
    lane = lax.broadcasted_iota(jnp.int32, block.shape, 1)
    return jnp.sum(jnp.where(lane == index, block, 0.0), axis=1, keepdims=True)


def encode(values):
    scale = jnp.max(jnp.abs(values), axis=1, keepdims=True)
    codes = jnp.floor(values * (CODE_TOP / jnp.maximum(scale, 1e-30)) + 0.5)
    return codes.astype(jnp.int32).astype(jnp.int16), scale * (1.0 / CODE_TOP)


def decode(codes):
    return codes.astype(jnp.int32).astype(jnp.float32)


def join_stats(top, total, scales):
    lane = lax.broadcasted_iota(jnp.int32, top.shape, 1)
    return jnp.where(lane < 16, top, jnp.where(lane < 32, pltpu.roll(total, 16, 1), scales))


def decode_kernel(
    meta_ref, q_ref, lat_ref, own_ref, gain_ref, table_ref, newtable_ref,
    out_ref, cache_ref,
    xbuf, lbuf, q_all, q_rows, partner, fresh, outgoing,
    states, state_stats, o_codes, stats,
    relay_in, direct_in, merged, merged_in, stat_in, mstat, mstat_in,
    zcodes, zin, zstat, zstat_in, values, out_f32,
    send_x, recv_x, send_q, recv_q, send_page, recv_page, send_role, recv_role,
    send_y, recv_y, send_z, recv_z, local_sem,
):
    role = lax.axis_index("role")
    group = lax.axis_index("grp")
    me = lax.axis_index("dev")
    z = me // RING_Y
    y = me % RING_Y
    up = (y + 1) % RING_Y
    down = (y + 3) % RING_Y
    far = (y + 2) % RING_Y
    rows = 8 * OWNERS
    pages = own_ref.shape[0]
    at_prefill = role == 0

    def at(zz, yy):
        return (role, group, zz * RING_Y + yy)

    other_core = (1 - role, group, me)
    neighbours = {
        "up": at(z, up),
        "down": at(z, down),
        "in": at((z + 1) % RING_Z, y),
        "out": at((z + 7) % RING_Z, y),
    }
    shards = [(role, (group + k) % 4, me) for k in range(1, 4)]
    greet(everyone(role, group, z, y) + shards + [other_core])
    copies = []

    def push(src, dst, sends, recvs, index, target):
        copy = pltpu.make_async_remote_copy(
            src_ref=src, dst_ref=dst, send_sem=sends.at[index], recv_sem=recvs.at[index],
            device_id=target, device_id_type=MESH_IDS,
        )
        copy.start()
        copies.append(copy)
        return copy

    arriving, arriving_latents = [], []
    for k in (2, 1, 3):
        target = (role, (group + k) % 4, me)
        arriving.append(push(q_ref, xbuf.at[group], send_x, recv_x, 2 * k, target))
    exchange = push(own_ref, partner, send_role, recv_role, OWNERS, other_core)
    for k in (2, 1, 3):
        target = (role, (group + k) % 4, me)
        arriving_latents.append(push(lat_ref, lbuf.at[group], send_x, recv_x, 2 * k + 1, target))
    xbuf[group] = q_ref[...]
    lbuf[group] = lat_ref[...]
    for copy in arriving:
        copy.wait_recv()

    def served(j):
        return meta_ref[SERVED + j]

    def pick(index):
        pair = xbuf[index // 12, (index % 12) // 2].astype(jnp.float32)
        return jnp.where(index % 2 == 0, pair[:8], pair[8:])

    for p in range(6):
        both = jnp.concatenate([pick(served(2 * p)), pick(served(2 * p + 1))], axis=0)
        q_all[me, 16 * p : 16 * p + 16, :] = both.astype(jnp.bfloat16)

    def slot(dz, dy):
        return ((z - dz + 2 * RING_Z) % RING_Z) * RING_Y + (y - dy + 2 * RING_Y) % RING_Y

    waits = {}

    def send(half, dz, dy, to):
        span = pl.ds(48 * half, 48)
        place = slot(dz, dy)
        ndz = dz + {"in": 1, "out": -1}.get(to, 0)
        ndy = dy + {"up": 1, "down": -1}.get(to, 0)
        index = half * 32 + (ndz % RING_Z) * RING_Y + ndy % RING_Y
        block = q_all.at[place, span]
        push(block, block, send_q, recv_q, index, neighbours[to])
        here = q_all.at[slot(ndz, ndy), span]
        waits[half, ndz, ndy] = pltpu.make_async_remote_copy(
            src_ref=here, dst_ref=here, send_sem=send_q.at[index], recv_sem=recv_q.at[index],
            device_id=neighbours[to], device_id_type=MESH_IDS,
        )
        return (half, ndz, ndy)

    def z_steps(half, dz, dy):
        deep = 4 if (half == 0 or dy in (0, 1)) else 3
        steps = []
        if 0 <= dz < deep:
            steps.append("in")
        if 0 >= dz > deep - 7:
            steps.append("out")
        return steps

    def y_steps(half, dz, dy):
        if dy == 0:
            return ["up", "down"]
        if dy == 1 and (half == 1 or dz % 2 == 0):
            return ["up"]
        if dy == -1 and half == 0 and dz % 2 == 1:
            return ["down"]
        return []

    def forward(block):
        half, dz, dy = block
        if half == 0:
            steps = (z_steps(half, dz, dy) if dy == 0 else []) + y_steps(half, dz, dy)
        else:
            steps = (y_steps(half, dz, dy) if dz == 0 else []) + z_steps(half, dz, dy)
        return [send(half, dz, dy, to) for to in steps]

    def advance(frontier):
        later = []
        for block in frontier:
            waits[block].wait_recv()
            later = later + forward(block)
        return later

    frontier = forward((0, 0, 0)) + forward((1, 0, 0))

    exchange.wait_recv()
    gain = gain_ref[...]

    def finish(raw, table):
        latent = raw[:, :LAT]
        mean_square = jnp.sum(latent * latent, axis=-1, keepdims=True) * (1.0 / LAT)
        normed = latent * lax.rsqrt(mean_square + epsilon) * gain
        rope = raw[:, LAT:]
        swapped = jnp.concatenate([rope[:, 32:], rope[:, :32]], axis=-1)
        turned = rope * table[:, :64] + swapped * table[:, 64:]
        return jnp.concatenate([normed, turned], axis=-1).astype(jnp.bfloat16)

    def one_page(i, _):
        raw = jnp.where(at_prefill, own_ref[i], partner[i]).astype(jnp.float32)
        fresh[i] = finish(raw, table_ref[i])
        return 0

    third = pages // 3
    for part in range(3):
        lax.fori_loop(part * third, (part + 1) * third, one_page, 0)
        if part < 2:
            frontier = advance(frontier)

    def one_slot(t, _):
        page = meta_ref[INVERSE + t]
        found = fresh[jnp.maximum(page, 0)]
        outgoing[t] = jnp.where(page >= 0, found, jnp.zeros_like(found))
        return 0

    lax.fori_loop(0, OWNERS, one_slot, 0)
    frontier = advance(frontier)

    sent_pages = DISTANCES[:-1]
    landing = []
    over = []

    def send_pages(first, last):
        for i in range(first, last):
            dz, dy = sent_pages[i]
            there = ((z + dz) % RING_Z) * RING_Y + (y + dy) % RING_Y
            landing.append(
                push(
                    outgoing.at[there], cache_ref.at[me, role], send_page, recv_page, i,
                    (role, group, there),
                )
            )

    def hand_over(first, last):
        for i in range(first, last):
            dz, dy = sent_pages[i]
            landing[i].wait_recv()
            page = cache_ref.at[slot(dz, dy), role]
            over.append(push(page, page, send_role, recv_role, i, other_core))

    send_pages(0, EARLY)
    keep_own = pltpu.make_async_copy(outgoing.at[me], cache_ref.at[me, role], local_sem)
    keep_own.start()
    over.append(
        push(outgoing.at[me], cache_ref.at[me, role], send_role, recv_role, OWNERS - 1, other_core)
    )
    while frontier:
        frontier = advance(frontier)
    send_pages(EARLY, BEFORE_ATTENTION)

    def order_rows(p, _):
        for yy in range(RING_Y):
            blocks = [
                q_all[zz * RING_Y + yy, pl.ds(pl.multiple_of(16 * p, 16), 16), :].astype(jnp.float32)
                for zz in range(RING_Z)
            ]
            for jj in range(2):
                picked = jnp.concatenate([block[jj * 8 : jj * 8 + 8] for block in blocks], axis=0)
                q_rows[2 * p + jj, yy * 64 : yy * 64 + 64, :] = picked.astype(jnp.bfloat16)
        return 0

    lax.fori_loop(0, 6, order_rows, 0)

    lane = lax.broadcasted_iota(jnp.int32, (rows, 2 * PAGE), 1)
    low = lane < PAGE
    step_of_row = (lax.broadcasted_iota(jnp.int32, (rows, 2 * PAGE), 0) % 8) // 2

    def score(q, keys):
        s = lax.dot_general(q, keys, (((1,), (1,)), ((), ())), preferred_element_type=jnp.float32)
        return s * logit_scale_factor

    states[0] = jnp.zeros((rows, LAT), jnp.float32)
    state_stats[0] = jnp.zeros((rows, 2), jnp.float32)
    page_lane = lax.broadcasted_iota(jnp.int32, (rows, PAGE), 1)

    def page_terms(x):
        request = meta_ref[REQUEST + x]
        keys = jnp.where(at_prefill, partner[x], own_ref[x])
        visible = page_lane < meta_ref[VALID + x]
        s = jnp.where(visible, score(q_rows[request], keys), lowest)
        m = jnp.max(s, axis=1, keepdims=True)
        e = jnp.where(visible, jnp.exp(s - m), 0.0)
        l = jnp.sum(e, axis=1, keepdims=True)
        o = jnp.dot(e.astype(jnp.bfloat16), keys[:, :LAT], preferred_element_type=jnp.float32)
        return m, l, o

    def chain(x, terms):
        m, l, o = terms
        same = meta_ref[SAME + x] == 1
        before = state_stats[x]
        m_before = jnp.where(same, before[:, 0:1], lowest)
        m_now = jnp.maximum(m, m_before)
        carry = jnp.where(same, jnp.exp(m_before - m_now), 0.0)
        f = jnp.exp(m - m_now)
        l_now = before[:, 1:2] * carry + l * f
        state_stats[x + 1] = jnp.concatenate([m_now, l_now], axis=1)
        states[x + 1] = states[x] * carry + o * f

    def two_resident(i, _):
        terms = [page_terms(2 * i), page_terms(2 * i + 1)]
        chain(2 * i, terms[0])
        chain(2 * i + 1, terms[1])
        return 0

    lax.fori_loop(0, pages // 2, two_resident, 0)

    for copy in arriving_latents:
        copy.wait_recv()

    mine = served(jnp.minimum(me, 11))
    new_raw = lbuf[mine // 12, (mine % 12) // 4].astype(jnp.float32)
    new_keys = finish(new_raw, newtable_ref[...])
    new_keys = jnp.concatenate(
        [new_keys, jnp.zeros((2 * PAGE - 16, KDIM), jnp.bfloat16)], axis=0
    )
    new_visible = (lane // 4 == mine % 4) & (lane % 4 <= step_of_row)

    def weigh(q, keys):
        s = score(q, keys)
        m1 = jnp.max(jnp.where(low, s, lowest), axis=1, keepdims=True)
        m2 = jnp.max(jnp.where(low, lowest, s), axis=1, keepdims=True)
        mb = jnp.where(low, m1, m2)
        e = jnp.exp(s - mb)
        m_now = jnp.maximum(m1, m2)
        f = jnp.exp(mb - m_now)
        l = jnp.sum(e * f, axis=1, keepdims=True)
        wide = e.astype(jnp.bfloat16).astype(jnp.float32) * f
        hi = wide.astype(jnp.bfloat16)
        lo = (wide - hi.astype(jnp.float32)).astype(jnp.bfloat16)
        v = keys[:, :LAT]
        o = jnp.dot(
            jnp.concatenate([hi, lo], axis=1),
            jnp.concatenate([v, v], axis=0),
            preferred_element_type=jnp.float32,
        )
        return m_now, l, o

    def whole_request(c, j):
        keys = fresh[pl.ds(2 * j, 2)].reshape(2 * PAGE, KDIM)
        m, l, o = weigh(q_rows[j], keys)
        last = meta_ref[END + j]
        has = meta_ref[END + j] > meta_ref[BEGIN + j]
        state = state_stats[last]
        m_state = jnp.where(has, state[:, 0:1], lowest)
        m_now = jnp.maximum(m, m_state)
        f = jnp.exp(m - m_now)
        g = jnp.where(has, jnp.exp(m_state - m_now), 0.0)
        l_now = l * f + state[:, 1:2] * g
        codes, scale = encode(o * f + states[last] * g)
        o_codes[:, j] = codes.reshape(RING_Y, rows // RING_Y, LAT)
        put_stats(c, j, m_now, l_now, scale)

        @pl.when(j == me)
        def _():
            s = jnp.where(new_visible, score(q_rows[j], new_keys), lowest)
            m_new = jnp.max(s, axis=1, keepdims=True)
            e = jnp.where(new_visible, jnp.exp(s - m_new), 0.0)
            l_new = jnp.sum(e, axis=1, keepdims=True)
            o_new = jnp.dot(
                e.astype(jnp.bfloat16), new_keys[:, :LAT], preferred_element_type=jnp.float32
            )
            m_all = jnp.maximum(m_now, m_new)
            old = jnp.exp(m_now - m_all)
            fresh_part = jnp.exp(m_new - m_all)
            mixed = (o * f + states[last] * g) * old + o_new * fresh_part
            codes, scale = encode(mixed)
            o_codes[:, j] = codes.reshape(RING_Y, rows // RING_Y, LAT)
            put_stats(c, j, m_all, l_now * old + l_new * fresh_part, scale)

    def put_stats(c, j, m, l, scale):
        block = stats[c].reshape(rows, 128)
        block = jnp.where(lane == 16 + j, l, jnp.where(lane == 32 + j, scale, block))
        stats[c] = jnp.where(lane == j, m, block).reshape(RING_Y, rows // RING_Y, 128)

    ways = (up, down)
    stat_far, stat_near, relayed, direct = {}, {}, {}, {}
    for c in range(CHUNKS):
        stats[c] = jnp.zeros((RING_Y, rows // RING_Y, 128), jnp.float32)

        def two_requests(i, _, c=c):
            whole_request(c, HALF * c + i)
            whole_request(c, 6 + HALF * c + i)
            return 0

        lax.fori_loop(0, HALF, two_requests, 0)
        for way, ahead in enumerate(ways):
            base = 6 * way + HALF * c
            first = 8 * c + 2 * way
            stat_far[c, way] = push(
                stats.at[c, far], stat_in.at[c, 2 * way], send_y, recv_y, first, at(z, ahead)
            )
            relayed[c, way] = push(
                o_codes.at[far, pl.ds(base, HALF)], relay_in.at[way, c], send_y, recv_y,
                first + 1, at(z, ahead),
            )
        for way, ahead in enumerate(ways):
            base = 6 * (1 - way) + HALF * c
            first = 8 * c + 4 + 2 * way
            stat_near[c, way] = push(
                stats.at[c, ahead], stat_in.at[c, 2 * way + 1], send_y, recv_y, first, at(z, ahead)
            )
            direct[c, way] = push(
                o_codes.at[ahead, pl.ds(base, HALF)], direct_in.at[way, c], send_y, recv_y,
                first + 1, at(z, ahead),
            )

    send_pages(BEFORE_ATTENTION, len(sent_pages))
    passed, passed_stat = {}, {}
    for c in range(CHUNKS):
        for way, ahead in enumerate(ways):
            stat_far[c, way].wait_recv()
            relayed[c, way].wait_recv()
            top, total, weights = merge_stats([stat_in[c, 2 * way], stats[c, ahead]])
            base = 6 * way + HALF * c

            def relay_one(i, scales, way=way, c=c, base=base, ahead=ahead, weights=weights):
                mixed = decode(relay_in[way, c, i]) * column(weights[0], base + i)
                mixed = mixed + decode(o_codes[ahead, base + i]) * column(weights[1], base + i)
                codes, scale = encode(mixed)
                merged[way, c, i] = codes
                at_lane = lax.broadcasted_iota(jnp.int32, scales.shape, 1)
                return jnp.where(at_lane == 32 + base + i, scale, scales)

            scales = lax.fori_loop(0, HALF, relay_one, jnp.zeros_like(top))
            mstat[way, c] = join_stats(top, total, scales)
            first = 8 * CHUNKS + 4 * c + 2 * way
            passed[c, way] = push(
                merged.at[way, c], merged_in.at[way, c], send_y, recv_y, first, at(z, ahead)
            )
            passed_stat[c, way] = push(
                mstat.at[way, c], mstat_in.at[way, c], send_y, recv_y, first + 1, at(z, ahead)
            )

    hand_over(0, 8)
    arrivals = {}
    for c in range(CHUNKS):
        merged_stats = []
        for way in range(2):
            stat_near[c, 1 - way].wait_recv()
            passed_stat[c, way].wait_recv()
            passed[c, way].wait_recv()
            direct[c, 1 - way].wait_recv()
            merged_stats.append(
                merge_stats([stats[c, y], mstat_in[way, c], stat_in[c, 2 * (1 - way) + 1]])
            )
        small = lax.broadcasted_iota(jnp.int32, (64, 128), 1)
        scales = jnp.zeros((64, 128), jnp.float32)
        for way in range(2):
            base = 6 * way + HALF * c
            weights = merged_stats[way][2]

            def land_one(i, scales, way=way, c=c, base=base, weights=weights):
                mixed = decode(o_codes[y, base + i]) * column(weights[0], base + i)
                mixed = mixed + decode(merged_in[way, c, i]) * column(weights[1], base + i)
                mixed = mixed + decode(direct_in[1 - way, c, i]) * column(weights[2], base + i)
                scale = jnp.maximum(jnp.max(jnp.abs(mixed), axis=1, keepdims=True), 1e-30)
                values[way * HALF + i] = jnp.floor(mixed * (CODE_TOP / scale) + 0.5)
                return jnp.where(small == 32 + base + i, scale * (1.0 / CODE_TOP), scales)

            scales = lax.fori_loop(0, HALF, land_one, scales)
        use_up = (small % 16) < 6
        top = jnp.where(use_up, merged_stats[0][0], merged_stats[1][0])
        total = jnp.where(use_up, merged_stats[0][1], merged_stats[1][1])
        zstat[c] = join_stats(top, total, scales)

        def split_one(zz, _, c=c):
            part = values[:, pl.ds(pl.multiple_of(zz * 8, 8), 8), :]
            part = part.reshape(2 * HALF * 8, LAT)
            zcodes[c, zz] = part.astype(jnp.int32).astype(jnp.int16)
            return 0

        lax.fori_loop(0, RING_Z, split_one, 0)
        for k in (4, 3, 5, 2, 6, 1, 7):
            there = (z + k) % RING_Z
            index = 2 * (c * RING_Z + k)
            arrivals[c, k] = (
                push(
                    zstat.at[c, pl.ds(there * 8, 8)], zstat_in.at[c, k], send_z, recv_z, index + 1,
                    at(there, y),
                ),
                push(zcodes.at[c, there], zin.at[c, k], send_z, recv_z, index, at(there, y)),
            )

    hand_over(8, len(sent_pages))
    for c in range(CHUNKS):
        for k in range(1, RING_Z):
            for copy in arrivals[c, k]:
                copy.wait_recv()
        finished = []
        blocks = [zstat[c, pl.ds(pl.multiple_of(z * 8, 8), 8), :]]
        blocks = blocks + [zstat_in[c, k] for k in range(1, RING_Z)]
        top, total, weights = merge_stats(blocks)
        for way in range(2):
            base = 6 * way + HALF * c
            sums = [1.0 / column(total, base + i) for i in range(HALF)]
            mixed = None
            for k in range(RING_Z):
                codes = zcodes.at[c, z] if k == 0 else zin.at[c, k]
                part = decode(codes[...])[way * HALF * 8 : (way + 1) * HALF * 8]
                factor = jnp.concatenate(
                    [column(weights[k], base + i) * sums[i] for i in range(HALF)], axis=0
                )
                mixed = part * factor if mixed is None else mixed + part * factor
            finished.append((base, mixed))
        for base, mixed in finished:
            out_f32[base * 8 : (base + HALF) * 8, :] = mixed
    out_ref[...] = out_f32[...].astype(jnp.bfloat16)
    keep_own.wait()
    for copy in over:
        copy.wait_recv()
    for copy in copies:
        copy.wait_send()


def decode_step(meta, queries, latents, own, gain, table, newtable):
    smem = pl.BlockSpec(memory_space=pltpu.SMEM)
    vmem = pl.BlockSpec(memory_space=pltpu.VMEM)
    hbm = pl.BlockSpec(memory_space=pl.ANY)
    pages = own.shape[0]
    rows = 8 * OWNERS
    half = (2, CHUNKS, HALF, 64, LAT)
    bf16, f32, i16 = jnp.bfloat16, jnp.float32, jnp.int16
    dma = pltpu.SemaphoreType.DMA
    return pl.pallas_call(
        decode_kernel,
        out_shape=(
            jax.ShapeDtypeStruct((96, LAT), bf16),
            jax.ShapeDtypeStruct((OWNERS, 2, PAGE, KDIM), bf16),
        ),
        in_specs=[smem, vmem, vmem, vmem, vmem, vmem, vmem],
        out_specs=(vmem, hbm),
        scratch_shapes=[
            pltpu.VMEM((4, 6, 16, KDIM), bf16),
            pltpu.VMEM((4, 3, 16, KDIM), bf16),
            pltpu.VMEM((OWNERS, 96, KDIM), bf16),
            pltpu.VMEM((12, rows, KDIM), bf16),
            pltpu.VMEM((pages, PAGE, KDIM), bf16),
            pltpu.VMEM((pages, PAGE, KDIM), bf16),
            pltpu.VMEM((OWNERS, PAGE, KDIM), bf16),
            pltpu.VMEM((pages + 1, rows, LAT), f32),
            pltpu.VMEM((pages + 1, rows, 2), f32),
            pltpu.VMEM((RING_Y, 12, rows // RING_Y, LAT), i16),
            pltpu.VMEM((CHUNKS, RING_Y, rows // RING_Y, 128), f32),
            pltpu.VMEM(half, i16),
            pltpu.VMEM(half, i16),
            pltpu.VMEM(half, i16),
            pltpu.VMEM(half, i16),
            pltpu.VMEM((CHUNKS, 4, 64, 128), f32),
            pltpu.VMEM((2, CHUNKS, 64, 128), f32),
            pltpu.VMEM((2, CHUNKS, 64, 128), f32),
            pltpu.VMEM((CHUNKS, RING_Z, 16 * HALF, LAT), i16),
            pltpu.VMEM((CHUNKS, RING_Z, 16 * HALF, LAT), i16),
            pltpu.VMEM((CHUNKS, 64, 128), f32),
            pltpu.VMEM((CHUNKS, RING_Z, 8, 128), f32),
            pltpu.VMEM((2 * HALF, 64, LAT), f32),
            pltpu.VMEM((96, LAT), f32),
            dma((8,)),
            dma((8,)),
            dma((64,)),
            dma((64,)),
            dma((OWNERS,)),
            dma((OWNERS,)),
            dma((OWNERS + 1,)),
            dma((OWNERS + 1,)),
            dma((12 * CHUNKS,)),
            dma((12 * CHUNKS,)),
            dma((2 * CHUNKS * RING_Z,)),
            dma((2 * CHUNKS * RING_Z,)),
            dma,
        ],
        compiler_params=pltpu.CompilerParams(
            vmem_limit_bytes=VMEM_LIMIT, collective_id=1, has_side_effects=True
        ),
        cost_estimate=pl.CostEstimate(
            flops=2_000_000_000, bytes_accessed=100_000_000, transcendentals=0
        ),
        name="decode_step",
    )(meta, queries, latents, own, gain.reshape(1, LAT), table, newtable)


def per_device(
    pool_pages,
    kv_gain,
    queries,
    decode_latent,
    served_request,
    resident_pages,
    resident_tail,
    page_dest,
):
    role = lax.axis_index("role")
    group = lax.axis_index("grp")
    owner = lax.axis_index("dev")
    own = pool_pages[0, 0, 0]
    pages_dev = own.shape[0]
    counts = resident_pages[0]
    tail_len = resident_tail[0]
    req_grp = counts.shape[0]
    steps = queries.shape[1]
    heads_here = queries.shape[2]
    per_prompt = pages_dev // req_grp
    span_len = per_prompt * PAGE * OWNERS
    res_len = PAGE * (counts - 1) + tail_len
    page_ids = jnp.arange(pages_dev, dtype=jnp.int32)
    positions = (
        res_len[:, None, None]
        + ((owner * per_prompt + jnp.arange(per_prompt, dtype=jnp.int32)) * PAGE)[None, :, None]
        + jnp.arange(PAGE, dtype=jnp.int32)[None, None, :]
    ).reshape(pages_dev, PAGE)
    mine = jnp.minimum(owner, req_grp - 1)
    my_len = jnp.sum(jnp.where(jnp.arange(req_grp) == mine, res_len, 0))
    new_positions = my_len + span_len + jnp.arange(16, dtype=jnp.int32) % steps

    targets = lax.dynamic_index_in_dim(page_dest[0], owner, 0, keepdims=False)
    wanted = jnp.arange(OWNERS, dtype=jnp.int32) * 2 + role
    hits = targets[None, :] == wanted[:, None]
    inverse = jnp.max(jnp.where(hits, page_ids[None, :], -1), axis=1)
    ids = jnp.arange(req_grp, dtype=jnp.int32)
    run_ends = jnp.sum(jnp.where(ids[None, :] <= ids[:, None], counts[None, :], 0), axis=1)
    starts = run_ends - counts
    flat = page_ids * OWNERS + owner
    begin = jnp.sum((flat[None, :] < starts[:, None]).astype(jnp.int32), axis=1)
    end = jnp.sum((flat[None, :] < run_ends[:, None]).astype(jnp.int32), axis=1)
    res_req = jnp.sum((flat[:, None] >= run_ends[None, :]).astype(jnp.int32), axis=1)
    whose = res_req[:, None] == ids[None, :]
    last_page = jnp.sum(jnp.where(whose, run_ends[None, :] - 1, 0), axis=1)
    last_tail = jnp.sum(jnp.where(whose, tail_len[None, :], 0), axis=1)
    valid = jnp.where(flat < last_page, PAGE, last_tail)
    first_of = jnp.sum(jnp.where(whose, begin[None, :], 0), axis=1)
    same = (page_ids > first_of).astype(jnp.int32)
    serving = lax.dynamic_slice_in_dim(served_request, group * req_grp, req_grp)
    meta = jnp.concatenate([serving, begin, end, res_req, valid, same, inverse]).astype(jnp.int32)

    attention, received = decode_step(
        meta, queries.reshape(6, 16, KDIM), decode_latent.reshape(3, 16, KDIM), own, kv_gain,
        rope_table(positions), rope_table(new_positions),
    )
    attention = attention.reshape(req_grp, steps, heads_here, LAT)
    received = received.reshape(1, 1, 2 * OWNERS, PAGE, KDIM)
    return (attention, received)


def solution(mesh):
    in_specs = (
        P("role", "grp", "dev", None, None, None),
        P(),
        P("grp", None, ("role", "dev"), None),
        P("grp", None, None),
        P(),
        P("grp", None),
        P("grp", None),
        P("grp", None, None),
    )
    out_specs = (P("grp", None, ("role", "dev"), None), P("grp", "dev", None, None, None))
    return jax.shard_map(
        per_device, mesh=mesh, in_specs=in_specs, out_specs=out_specs, check_vma=False
    )
```

```python
import functools

import jax
import jax.numpy as jnp
from jax import lax
from jax.experimental import pallas as pl
from jax.experimental.pallas import tpu as pltpu
from jax.sharding import PartitionSpec as P

logit_scale_factor = 192.0 ** (-0.5)
epsilon = 1e-06
lowest = -1e30

VMEM_LIMIT = 58 * 1024 * 1024
LAT = 512
KDIM = 576
PAGE = 64
OWNERS = 32
RING_Y = 4
RING_Z = 8


BEGIN, END, RUN_END, REQUEST, VALID, SAME, INVERSE = 0, 12, 24, 36, 60, 84, 108


def rope_table(positions, frequency):
    lane = lax.broadcasted_iota(jnp.int32, positions.shape, 1)
    angles = positions.astype(jnp.float32) * frequency
    sine_part = jnp.sin(angles)
    turned = jnp.where(lane < 96, -sine_part, sine_part)
    return jnp.where(lane < 64, jnp.cos(angles), turned)


MESH_IDS = pl.DeviceIdType.MESH
CODE_TOP = 32767.0
CHUNKS = 3
HALF = 6 // CHUNKS


DISTANCES = [(0, dy) for dy in (2, 1, 3)]
DISTANCES = DISTANCES + [(dz, dy) for dy in (1, 3, 2, 0) for dz in (4, 3, 5, 2, 6, 1, 7)]
DISTANCES = DISTANCES + [(0, 0)]
EARLY, BEFORE_ATTENTION = 0, 20


def everyone(role, group, z, y):
    return [
        (role, group, ((z + dz) % RING_Z) * RING_Y + (y + dy) % RING_Y)
        for dz, dy in DISTANCES
        if (dz, dy) != (0, 0)
    ]


def greet(devices):
    barrier = pltpu.get_barrier_semaphore()
    for device in devices:
        pl.semaphore_signal(barrier, inc=1, device_id=device, device_id_type=MESH_IDS)
    pl.semaphore_wait(barrier, len(devices))


def merge_stats(blocks):
    lane = lax.broadcasted_iota(jnp.int32, blocks[0].shape, 1)
    top = functools.reduce(jnp.maximum, blocks)
    total = jnp.zeros_like(top)
    weights = []
    for block in blocks:
        part = jnp.exp(jnp.where(lane < 16, block - top, 0.0))
        total = total + part * pltpu.roll(block, 112, 1)
        weights.append(part * pltpu.roll(block, 96, 1))
    return top, total, weights


def column(block, index):
    lane = lax.broadcasted_iota(jnp.int32, block.shape, 1)
    return jnp.sum(jnp.where(lane == index, block, 0.0), axis=1, keepdims=True)


def encode(values):
    scale = jnp.max(jnp.abs(values), axis=1, keepdims=True)
    codes = jnp.floor(values * (CODE_TOP / jnp.maximum(scale, 1e-30)) + 0.5)
    return codes.astype(jnp.int32).astype(jnp.int16), scale * (1.0 / CODE_TOP)


def decode(codes):
    return codes.astype(jnp.int32).astype(jnp.float32)


def join_stats(top, total, scales):
    lane = lax.broadcasted_iota(jnp.int32, top.shape, 1)
    return jnp.where(lane < 16, top, jnp.where(lane < 32, pltpu.roll(total, 16, 1), scales))


def decode_kernel(
    served_ref, counts_ref, tail_ref, dest_ref, q_ref, lat_ref, own_ref, gain_ref, frequency_ref,
    out_ref, cache_ref,
    meta_ref, table,
    xbuf, lbuf, q_all, q_rows, partner, fresh, outgoing,
    states, state_m, state_l, o_codes, stats,
    relay_in, direct_in, merged, merged_in, stat_in, mstat, mstat_in,
    zcodes, zin, zstat, zstat_in, values, out_f32,
    send_x, recv_x, send_q, recv_q, send_page, recv_page, send_role, recv_role,
    send_y, recv_y, send_z, recv_z, local_sem,
):
    role = lax.axis_index("role")
    group = lax.axis_index("grp")
    me = lax.axis_index("dev")
    z = me // RING_Y
    y = me % RING_Y
    up = (y + 1) % RING_Y
    down = (y + 3) % RING_Y
    far = (y + 2) % RING_Y
    rows = 8 * OWNERS
    pages = own_ref.shape[0]
    at_prefill = role == 0

    def at(zz, yy):
        return (role, group, zz * RING_Y + yy)

    other_core = (1 - role, group, me)
    neighbours = {
        "up": at(z, up),
        "down": at(z, down),
        "in": at((z + 1) % RING_Z, y),
        "out": at((z + 7) % RING_Z, y),
    }
    shards = [(role, (group + k) % 4, me) for k in range(1, 4)]
    greet(everyone(role, group, z, y) + shards + [other_core])
    copies = []

    def push(src, dst, sends, recvs, index, target):
        copy = pltpu.make_async_remote_copy(
            src_ref=src, dst_ref=dst, send_sem=sends.at[index], recv_sem=recvs.at[index],
            device_id=target, device_id_type=MESH_IDS,
        )
        copy.start()
        copies.append(copy)
        return copy

    arriving, arriving_latents = [], []
    for k in (2, 1, 3):
        target = (role, (group + k) % 4, me)
        arriving.append(push(q_ref, xbuf.at[group], send_x, recv_x, 2 * k, target))
    exchange = push(own_ref, partner, send_role, recv_role, OWNERS, other_core)
    for k in (2, 1, 3):
        target = (role, (group + k) % 4, me)
        arriving_latents.append(push(lat_ref, lbuf.at[group], send_x, recv_x, 2 * k + 1, target))
    xbuf[group] = q_ref[...]
    lbuf[group] = lat_ref[...]

    def served(j):
        return served_ref[group * 12 + j]

    def context(j):
        return PAGE * (counts_ref[0, j] - 1) + tail_ref[0, j]

    run = 0
    for j in range(12):
        meta_ref[BEGIN + j] = (run - me + OWNERS - 1) // OWNERS
        run = run + counts_ref[0, j]
        meta_ref[END + j] = (run - me + OWNERS - 1) // OWNERS
        meta_ref[RUN_END + j] = run

    def describe(x, _):
        flat = x * OWNERS + me
        request = 0
        for j in range(11):
            request = request + (flat >= meta_ref[RUN_END + j]).astype(jnp.int32)
        meta_ref[REQUEST + x] = request
        meta_ref[VALID + x] = jnp.where(
            flat < meta_ref[RUN_END + request] - 1, PAGE, tail_ref[0, request]
        )
        meta_ref[SAME + x] = (x > meta_ref[BEGIN + request]).astype(jnp.int32)
        return 0

    lax.fori_loop(0, pages, describe, 0)

    def invert(t, _):
        page = -1
        for i in range(24):
            page = jnp.where(dest_ref[me, i] == 2 * t + role, i, page)
        meta_ref[INVERSE + t] = page
        return 0

    lax.fori_loop(0, OWNERS, invert, 0)
    frequency = frequency_ref[...]
    token = lax.broadcasted_iota(jnp.int32, (PAGE, 128), 0)

    def one_table(i, _):
        base = context(i // 2) + (me * 2 + i % 2) * PAGE
        table[i] = rope_table(base + token, frequency)
        return 0

    lax.fori_loop(0, pages, one_table, 0)
    new_base = context(jnp.minimum(me, 11)) + 2 * OWNERS * PAGE
    new_table = rope_table(new_base + token[:16] % 4, frequency)
    for copy in arriving:
        copy.wait_recv()

    def pick(index):
        pair = xbuf[index // 12, (index % 12) // 2].astype(jnp.float32)
        return jnp.where(index % 2 == 0, pair[:8], pair[8:])

    for p in range(6):
        both = jnp.concatenate([pick(served(2 * p)), pick(served(2 * p + 1))], axis=0)
        q_all[me, 16 * p : 16 * p + 16, :] = both.astype(jnp.bfloat16)

    def slot(dz, dy):
        return ((z - dz + 2 * RING_Z) % RING_Z) * RING_Y + (y - dy + 2 * RING_Y) % RING_Y

    waits = {}

    def send(half, dz, dy, to):
        span = pl.ds(48 * half, 48)
        place = slot(dz, dy)
        ndz = dz + {"in": 1, "out": -1}.get(to, 0)
        ndy = dy + {"up": 1, "down": -1}.get(to, 0)
        index = half * 32 + (ndz % RING_Z) * RING_Y + ndy % RING_Y
        block = q_all.at[place, span]
        push(block, block, send_q, recv_q, index, neighbours[to])
        here = q_all.at[slot(ndz, ndy), span]
        waits[half, ndz, ndy] = pltpu.make_async_remote_copy(
            src_ref=here, dst_ref=here, send_sem=send_q.at[index], recv_sem=recv_q.at[index],
            device_id=neighbours[to], device_id_type=MESH_IDS,
        )
        return (half, ndz, ndy)

    def z_steps(half, dz, dy):
        deep = 4 if (half == 0 or dy in (0, 1)) else 3
        steps = []
        if 0 <= dz < deep:
            steps.append("in")
        if 0 >= dz > deep - 7:
            steps.append("out")
        return steps

    def y_steps(half, dz, dy):
        if dy == 0:
            return ["up", "down"]
        if dy == 1 and (half == 1 or dz % 2 == 0):
            return ["up"]
        if dy == -1 and half == 0 and dz % 2 == 1:
            return ["down"]
        return []

    def forward(block):
        half, dz, dy = block
        if half == 0:
            steps = (z_steps(half, dz, dy) if dy == 0 else []) + y_steps(half, dz, dy)
        else:
            steps = (y_steps(half, dz, dy) if dz == 0 else []) + z_steps(half, dz, dy)
        return [send(half, dz, dy, to) for to in steps]

    def advance(frontier):
        later = []
        for block in frontier:
            waits[block].wait_recv()
            later = later + forward(block)
        return later

    frontier = forward((0, 0, 0)) + forward((1, 0, 0))

    exchange.wait_recv()
    gain = gain_ref[...]

    def finish(raw, turns):
        latent = raw[:, :LAT]
        mean_square = jnp.sum(latent * latent, axis=-1, keepdims=True) * (1.0 / LAT)
        normed = latent * lax.rsqrt(mean_square + epsilon) * gain
        rope = raw[:, LAT:]
        swapped = jnp.concatenate([rope[:, 32:], rope[:, :32]], axis=-1)
        turned = rope * turns[:, :64] + swapped * turns[:, 64:]
        return jnp.concatenate([normed, turned], axis=-1).astype(jnp.bfloat16)

    def one_page(i, _):
        raw = jnp.where(at_prefill, own_ref[i], partner[i]).astype(jnp.float32)
        fresh[i] = finish(raw, table[i])
        return 0

    third = pages // 3
    for part in range(3):
        lax.fori_loop(part * third, (part + 1) * third, one_page, 0)
        if part < 2:
            frontier = advance(frontier)

    def one_slot(t, _):
        page = meta_ref[INVERSE + t]
        found = fresh[jnp.maximum(page, 0)]
        outgoing[t] = jnp.where(page >= 0, found, jnp.zeros_like(found))
        return 0

    lax.fori_loop(0, OWNERS, one_slot, 0)
    frontier = advance(frontier)

    sent_pages = DISTANCES[:-1]
    landing = []
    over = []

    def send_pages(first, last):
        for i in range(first, last):
            dz, dy = sent_pages[i]
            there = ((z + dz) % RING_Z) * RING_Y + (y + dy) % RING_Y
            landing.append(
                push(
                    outgoing.at[there], cache_ref.at[me, role], send_page, recv_page, i,
                    (role, group, there),
                )
            )

    def hand_over(first, last):
        for i in range(first, last):
            dz, dy = sent_pages[i]
            landing[i].wait_recv()
            page = cache_ref.at[slot(dz, dy), role]
            over.append(push(page, page, send_role, recv_role, i, other_core))

    send_pages(0, EARLY)
    keep_own = pltpu.make_async_copy(outgoing.at[me], cache_ref.at[me, role], local_sem)
    keep_own.start()
    over.append(
        push(outgoing.at[me], cache_ref.at[me, role], send_role, recv_role, OWNERS - 1, other_core)
    )
    while frontier:
        frontier = advance(frontier)
    send_pages(EARLY, BEFORE_ATTENTION)

    def order_rows(p, _):
        for yy in range(RING_Y):
            blocks = [
                q_all[zz * RING_Y + yy, pl.ds(pl.multiple_of(16 * p, 16), 16), :].astype(jnp.float32)
                for zz in range(RING_Z)
            ]
            for jj in range(2):
                picked = jnp.concatenate([block[jj * 8 : jj * 8 + 8] for block in blocks], axis=0)
                q_rows[2 * p + jj, yy * 64 : yy * 64 + 64, :] = picked.astype(jnp.bfloat16)
        return 0

    lax.fori_loop(0, 6, order_rows, 0)

    lane = lax.broadcasted_iota(jnp.int32, (rows, 2 * PAGE), 1)
    low = lane < PAGE
    step_of_row = (lax.broadcasted_iota(jnp.int32, (rows, 2 * PAGE), 0) % 8) // 2

    def score(q, keys):
        s = lax.dot_general(q, keys, (((1,), (1,)), ((), ())), preferred_element_type=jnp.float32)
        return s * logit_scale_factor

    states[0] = jnp.zeros((rows, LAT), jnp.float32)
    state_m[0] = jnp.zeros((rows, 128), jnp.float32)
    state_l[0] = jnp.zeros((rows, 128), jnp.float32)
    page_lane = lax.broadcasted_iota(jnp.int32, (rows, PAGE), 1)

    def page_terms(x):
        request = meta_ref[REQUEST + x]
        keys = jnp.where(at_prefill, partner[x], own_ref[x])
        visible = page_lane < meta_ref[VALID + x]
        s = jnp.where(visible, score(q_rows[request], keys), lowest)
        m = jnp.max(s, axis=1, keepdims=True)
        e = jnp.where(visible, jnp.exp(s - m), 0.0)
        l = jnp.sum(e, axis=1, keepdims=True)
        o = jnp.dot(e.astype(jnp.bfloat16), keys[:, :LAT], preferred_element_type=jnp.float32)
        return m, l, o

    def wide(column_values):
        return jnp.broadcast_to(column_values, (rows, 128))

    def blend(left, a, right, b):
        tiles = [
            left[:, k : k + 128] * a + right[:, k : k + 128] * b for k in range(0, LAT, 128)
        ]
        return jnp.concatenate(tiles, axis=1)

    def chain(x, terms):
        m, l, o = terms
        same = meta_ref[SAME + x] == 1
        m = wide(m)
        m_before = jnp.where(same, state_m[x], lowest)
        m_now = jnp.maximum(m, m_before)
        carry = jnp.where(same, jnp.exp(m_before - m_now), 0.0)
        f = jnp.exp(m - m_now)
        state_m[x + 1] = m_now
        state_l[x + 1] = state_l[x] * carry + wide(l) * f
        states[x + 1] = blend(states[x], carry, o, f)

    def two_resident(i, _):
        terms = [page_terms(2 * i), page_terms(2 * i + 1)]
        chain(2 * i, terms[0])
        chain(2 * i + 1, terms[1])
        return 0

    lax.fori_loop(0, pages // 2, two_resident, 0)

    for copy in arriving_latents:
        copy.wait_recv()

    mine = served(jnp.minimum(me, 11))
    new_raw = lbuf[mine // 12, (mine % 12) // 4].astype(jnp.float32)
    new_keys = finish(new_raw, new_table)
    new_keys = jnp.concatenate(
        [new_keys, jnp.zeros((2 * PAGE - 16, KDIM), jnp.bfloat16)], axis=0
    )
    new_visible = (lane // 4 == mine % 4) & (lane % 4 <= step_of_row)

    def weigh(q, keys):
        s = score(q, keys)
        m1 = jnp.max(jnp.where(low, s, lowest), axis=1, keepdims=True)
        m2 = jnp.max(jnp.where(low, lowest, s), axis=1, keepdims=True)
        mb = jnp.where(low, m1, m2)
        e = jnp.exp(s - mb)
        m_now = jnp.maximum(m1, m2)
        f = jnp.exp(mb - m_now)
        l = jnp.sum(e * f, axis=1, keepdims=True)
        wide = e.astype(jnp.bfloat16).astype(jnp.float32) * f
        hi = wide.astype(jnp.bfloat16)
        lo = (wide - hi.astype(jnp.float32)).astype(jnp.bfloat16)
        v = keys[:, :LAT]
        o = jnp.dot(
            jnp.concatenate([hi, lo], axis=1),
            jnp.concatenate([v, v], axis=0),
            preferred_element_type=jnp.float32,
        )
        return m_now, l, o

    def whole_request(c, j):
        keys = fresh[pl.ds(2 * j, 2)].reshape(2 * PAGE, KDIM)
        m, l, o = weigh(q_rows[j], keys)
        last = meta_ref[END + j]
        has = meta_ref[END + j] > meta_ref[BEGIN + j]
        m = wide(m)
        m_state = jnp.where(has, state_m[last], lowest)
        m_now = jnp.maximum(m, m_state)
        f = jnp.exp(m - m_now)
        g = jnp.where(has, jnp.exp(m_state - m_now), 0.0)
        l_now = wide(l) * f + state_l[last] * g
        codes, scale = encode(blend(o, f, states[last], g))
        o_codes[:, j] = codes.reshape(RING_Y, rows // RING_Y, LAT)
        put_stats(c, j, m_now, l_now, scale)

        @pl.when(j == me)
        def _():
            s = jnp.where(new_visible, score(q_rows[j], new_keys), lowest)
            m_new = jnp.max(s, axis=1, keepdims=True)
            e = jnp.where(new_visible, jnp.exp(s - m_new), 0.0)
            l_new = jnp.sum(e, axis=1, keepdims=True)
            o_new = jnp.dot(
                e.astype(jnp.bfloat16), new_keys[:, :LAT], preferred_element_type=jnp.float32
            )
            m_new = wide(m_new)
            m_all = jnp.maximum(m_now, m_new)
            old = jnp.exp(m_now - m_all)
            fresh_part = jnp.exp(m_new - m_all)
            mixed = blend(blend(o, f, states[last], g), old, o_new, fresh_part)
            codes, scale = encode(mixed)
            o_codes[:, j] = codes.reshape(RING_Y, rows // RING_Y, LAT)
            put_stats(c, j, m_all, l_now * old + wide(l_new) * fresh_part, scale)

    def put_stats(c, j, m, l, scale):
        block = stats[c].reshape(rows, 128)
        block = jnp.where(lane == 16 + j, l, jnp.where(lane == 32 + j, scale, block))
        stats[c] = jnp.where(lane == j, m, block).reshape(RING_Y, rows // RING_Y, 128)

    ways = (up, down)
    stat_far, stat_near, relayed, direct = {}, {}, {}, {}
    def attend(c):
        stats[c] = jnp.zeros((RING_Y, rows // RING_Y, 128), jnp.float32)

        def two_requests(i, _, c=c):
            whole_request(c, HALF * c + i)
            whole_request(c, 6 + HALF * c + i)
            return 0

        lax.fori_loop(0, HALF, two_requests, 0)
        for way, ahead in enumerate(ways):
            base = 6 * way + HALF * c
            first = 8 * c + 2 * way
            stat_far[c, way] = push(
                stats.at[c, far], stat_in.at[c, 2 * way], send_y, recv_y, first, at(z, ahead)
            )
            relayed[c, way] = push(
                o_codes.at[far, pl.ds(base, HALF)], relay_in.at[way, c], send_y, recv_y,
                first + 1, at(z, ahead),
            )
        for way, ahead in enumerate(ways):
            base = 6 * (1 - way) + HALF * c
            first = 8 * c + 4 + 2 * way
            stat_near[c, way] = push(
                stats.at[c, ahead], stat_in.at[c, 2 * way + 1], send_y, recv_y, first, at(z, ahead)
            )
            direct[c, way] = push(
                o_codes.at[ahead, pl.ds(base, HALF)], direct_in.at[way, c], send_y, recv_y,
                first + 1, at(z, ahead),
            )

    passed, passed_stat = {}, {}
    def relay(c):
        for way, ahead in enumerate(ways):
            stat_far[c, way].wait_recv()
            relayed[c, way].wait_recv()
            top, total, weights = merge_stats([stat_in[c, 2 * way], stats[c, ahead]])
            base = 6 * way + HALF * c

            def relay_one(i, scales, way=way, c=c, base=base, ahead=ahead, weights=weights):
                mixed = decode(relay_in[way, c, i]) * column(weights[0], base + i)
                mixed = mixed + decode(o_codes[ahead, base + i]) * column(weights[1], base + i)
                codes, scale = encode(mixed)
                merged[way, c, i] = codes
                at_lane = lax.broadcasted_iota(jnp.int32, scales.shape, 1)
                return jnp.where(at_lane == 32 + base + i, scale, scales)

            scales = lax.fori_loop(0, HALF, relay_one, jnp.zeros_like(top))
            mstat[way, c] = join_stats(top, total, scales)
            first = 8 * CHUNKS + 4 * c + 2 * way
            passed[c, way] = push(
                merged.at[way, c], merged_in.at[way, c], send_y, recv_y, first, at(z, ahead)
            )
            passed_stat[c, way] = push(
                mstat.at[way, c], mstat_in.at[way, c], send_y, recv_y, first + 1, at(z, ahead)
            )

    arrivals = {}

    def land(c):
        merged_stats = []
        for way in range(2):
            stat_near[c, 1 - way].wait_recv()
            passed_stat[c, way].wait_recv()
            passed[c, way].wait_recv()
            direct[c, 1 - way].wait_recv()
            merged_stats.append(
                merge_stats([stats[c, y], mstat_in[way, c], stat_in[c, 2 * (1 - way) + 1]])
            )
        small = lax.broadcasted_iota(jnp.int32, (64, 128), 1)
        scales = jnp.zeros((64, 128), jnp.float32)
        for way in range(2):
            base = 6 * way + HALF * c
            weights = merged_stats[way][2]

            def land_one(i, scales, way=way, c=c, base=base, weights=weights):
                mixed = decode(o_codes[y, base + i]) * column(weights[0], base + i)
                mixed = mixed + decode(merged_in[way, c, i]) * column(weights[1], base + i)
                mixed = mixed + decode(direct_in[1 - way, c, i]) * column(weights[2], base + i)
                scale = jnp.maximum(jnp.max(jnp.abs(mixed), axis=1, keepdims=True), 1e-30)
                values[way * HALF + i] = jnp.floor(mixed * (CODE_TOP / scale) + 0.5)
                return jnp.where(small == 32 + base + i, scale * (1.0 / CODE_TOP), scales)

            scales = lax.fori_loop(0, HALF, land_one, scales)
        use_up = (small % 16) < 6
        top = jnp.where(use_up, merged_stats[0][0], merged_stats[1][0])
        total = jnp.where(use_up, merged_stats[0][1], merged_stats[1][1])
        zstat[c] = join_stats(top, total, scales)

        def split_one(zz, _, c=c):
            part = values[:, pl.ds(pl.multiple_of(zz * 8, 8), 8), :]
            part = part.reshape(2 * HALF * 8, LAT)
            zcodes[c, zz] = part.astype(jnp.int32).astype(jnp.int16)
            return 0

        lax.fori_loop(0, RING_Z, split_one, 0)
        for k in (4, 3, 5, 2, 6, 1, 7):
            there = (z + k) % RING_Z
            index = 2 * (c * RING_Z + k)
            arrivals[c, k] = (
                push(
                    zstat.at[c, pl.ds(there * 8, 8)], zstat_in.at[c, k], send_z, recv_z, index + 1,
                    at(there, y),
                ),
                push(zcodes.at[c, there], zin.at[c, k], send_z, recv_z, index, at(there, y)),
            )

    for c in range(CHUNKS):
        attend(c)
        if c >= 1:
            relay(c - 1)
    send_pages(BEFORE_ATTENTION, len(sent_pages))
    relay(CHUNKS - 1)
    hand_over(0, 8)
    for c in range(CHUNKS):
        land(c)
    hand_over(8, len(sent_pages))
    for c in range(CHUNKS):
        for k in range(1, RING_Z):
            for copy in arrivals[c, k]:
                copy.wait_recv()
        finished = []
        blocks = [zstat[c, pl.ds(pl.multiple_of(z * 8, 8), 8), :]]
        blocks = blocks + [zstat_in[c, k] for k in range(1, RING_Z)]
        top, total, weights = merge_stats(blocks)
        for way in range(2):
            base = 6 * way + HALF * c
            sums = [1.0 / column(total, base + i) for i in range(HALF)]
            mixed = None
            for k in range(RING_Z):
                codes = zcodes.at[c, z] if k == 0 else zin.at[c, k]
                part = decode(codes[...])[way * HALF * 8 : (way + 1) * HALF * 8]
                factor = jnp.concatenate(
                    [column(weights[k], base + i) * sums[i] for i in range(HALF)], axis=0
                )
                mixed = part * factor if mixed is None else mixed + part * factor
            finished.append((base, mixed))
        for base, mixed in finished:
            out_f32[base * 8 : (base + HALF) * 8, :] = mixed
    out_ref[...] = out_f32[...].astype(jnp.bfloat16)
    keep_own.wait()
    for copy in over:
        copy.wait_recv()
    for copy in copies:
        copy.wait_send()


def decode_step(served, counts, tails, dest, queries, latents, own, gain, frequency):
    smem = pl.BlockSpec(memory_space=pltpu.SMEM)
    vmem = pl.BlockSpec(memory_space=pltpu.VMEM)
    hbm = pl.BlockSpec(memory_space=pl.ANY)
    pages = own.shape[0]
    rows = 8 * OWNERS
    half = (2, CHUNKS, HALF, 64, LAT)
    bf16, f32, i16 = jnp.bfloat16, jnp.float32, jnp.int16
    dma = pltpu.SemaphoreType.DMA
    return pl.pallas_call(
        decode_kernel,
        out_shape=(
            jax.ShapeDtypeStruct((96, LAT), bf16),
            jax.ShapeDtypeStruct((OWNERS, 2, PAGE, KDIM), bf16),
        ),
        in_specs=[smem, smem, smem, smem, vmem, vmem, vmem, vmem, vmem],
        out_specs=(vmem, hbm),
        scratch_shapes=[
            pltpu.SMEM((144,), jnp.int32),
            pltpu.VMEM((pages, PAGE, 128), f32),
            pltpu.VMEM((4, 6, 16, KDIM), bf16),
            pltpu.VMEM((4, 3, 16, KDIM), bf16),
            pltpu.VMEM((OWNERS, 96, KDIM), bf16),
            pltpu.VMEM((12, rows, KDIM), bf16),
            pltpu.VMEM((pages, PAGE, KDIM), bf16),
            pltpu.VMEM((pages, PAGE, KDIM), bf16),
            pltpu.VMEM((OWNERS, PAGE, KDIM), bf16),
            pltpu.VMEM((pages + 1, rows, LAT), f32),
            pltpu.VMEM((pages + 1, rows, 128), f32),
            pltpu.VMEM((pages + 1, rows, 128), f32),
            pltpu.VMEM((RING_Y, 12, rows // RING_Y, LAT), i16),
            pltpu.VMEM((CHUNKS, RING_Y, rows // RING_Y, 128), f32),
            pltpu.VMEM(half, i16),
            pltpu.VMEM(half, i16),
            pltpu.VMEM(half, i16),
            pltpu.VMEM(half, i16),
            pltpu.VMEM((CHUNKS, 4, 64, 128), f32),
            pltpu.VMEM((2, CHUNKS, 64, 128), f32),
            pltpu.VMEM((2, CHUNKS, 64, 128), f32),
            pltpu.VMEM((CHUNKS, RING_Z, 16 * HALF, LAT), i16),
            pltpu.VMEM((CHUNKS, RING_Z, 16 * HALF, LAT), i16),
            pltpu.VMEM((CHUNKS, 64, 128), f32),
            pltpu.VMEM((CHUNKS, RING_Z, 8, 128), f32),
            pltpu.VMEM((2 * HALF, 64, LAT), f32),
            pltpu.VMEM((96, LAT), f32),
            dma((8,)),
            dma((8,)),
            dma((64,)),
            dma((64,)),
            dma((OWNERS,)),
            dma((OWNERS,)),
            dma((OWNERS + 1,)),
            dma((OWNERS + 1,)),
            dma((12 * CHUNKS,)),
            dma((12 * CHUNKS,)),
            dma((2 * CHUNKS * RING_Z,)),
            dma((2 * CHUNKS * RING_Z,)),
            dma,
        ],
        compiler_params=pltpu.CompilerParams(
            vmem_limit_bytes=VMEM_LIMIT, collective_id=1, has_side_effects=True
        ),
        cost_estimate=pl.CostEstimate(
            flops=2_000_000_000, bytes_accessed=100_000_000, transcendentals=0
        ),
        name="decode_step",
    )(served, counts, tails, dest, queries, latents, own, gain.reshape(1, LAT), frequency)


def per_device(
    pool_pages,
    kv_gain,
    queries,
    decode_latent,
    served_request,
    resident_pages,
    resident_tail,
    page_dest,
):
    own = pool_pages[0, 0, 0]
    req_grp = resident_pages.shape[1]
    steps = queries.shape[1]
    heads_here = queries.shape[2]
    frequency = 10000.0 ** (-(jnp.arange(128) % 32).astype(jnp.float32) / 32)
    attention, received = decode_step(
        served_request, resident_pages, resident_tail, page_dest[0],
        queries.reshape(6, 16, KDIM), decode_latent.reshape(3, 16, KDIM), own, kv_gain,
        frequency.reshape(1, 128),
    )
    attention = attention.reshape(req_grp, steps, heads_here, LAT)
    received = received.reshape(1, 1, 2 * OWNERS, PAGE, KDIM)
    return (attention, received)


def solution(mesh):
    in_specs = (
        P("role", "grp", "dev", None, None, None),
        P(),
        P("grp", None, ("role", "dev"), None),
        P("grp", None, None),
        P(),
        P("grp", None),
        P("grp", None),
        P("grp", None, None),
    )
    out_specs = (P("grp", None, ("role", "dev"), None), P("grp", "dev", None, None, None))
    return jax.shard_map(
        per_device, mesh=mesh, in_specs=in_specs, out_specs=out_specs, check_vma=False
    )
```

```python
import functools

import jax
import jax.numpy as jnp
from jax import lax
from jax.experimental import pallas as pl
from jax.experimental.pallas import tpu as pltpu
from jax.sharding import PartitionSpec as P

logit_scale_factor = 192.0 ** (-0.5)
epsilon = 1e-06
lowest = -1e30

VMEM_LIMIT = 58 * 1024 * 1024
LAT = 512
KDIM = 576
PAGE = 64
OWNERS = 32
RING_Y = 4
RING_Z = 8


BEGIN, END, RUN_END, REQUEST, VALID, SAME, INVERSE = 0, 12, 24, 36, 60, 84, 108


def rope_table(positions, frequency):
    lane = lax.broadcasted_iota(jnp.int32, positions.shape, 1)
    angles = positions.astype(jnp.float32) * frequency
    sine_part = jnp.sin(angles)
    turned = jnp.where(lane < 96, -sine_part, sine_part)
    return jnp.where(lane < 64, jnp.cos(angles), turned)


MESH_IDS = pl.DeviceIdType.MESH
CODE_TOP = 32767.0
CHUNKS = 3
HALF = 6 // CHUNKS


DISTANCES = [(0, dy) for dy in (2, 1, 3)]
DISTANCES = DISTANCES + [(dz, dy) for dz in (4, 3, 5, 2, 6, 1, 7) for dy in (2, 1, 3)]
DISTANCES = DISTANCES + [(dz, 0) for dz in (4, 3, 5, 2, 6, 1, 7)]
DISTANCES = DISTANCES + [(0, 0)]
EARLY, BEFORE_ATTENTION = 0, 31


def everyone(role, group, z, y):
    return [
        (role, group, ((z + dz) % RING_Z) * RING_Y + (y + dy) % RING_Y)
        for dz, dy in DISTANCES
        if (dz, dy) != (0, 0)
    ]


def greet(devices):
    barrier = pltpu.get_barrier_semaphore()
    for device in devices:
        pl.semaphore_signal(barrier, inc=1, device_id=device, device_id_type=MESH_IDS)
    pl.semaphore_wait(barrier, len(devices))


def merge_stats(blocks):
    lane = lax.broadcasted_iota(jnp.int32, blocks[0].shape, 1)
    top = functools.reduce(jnp.maximum, blocks)
    total = jnp.zeros_like(top)
    weights = []
    for block in blocks:
        part = jnp.exp(jnp.where(lane < 16, block - top, 0.0))
        total = total + part * pltpu.roll(block, 112, 1)
        weights.append(part * pltpu.roll(block, 96, 1))
    return top, total, weights


def column(block, index):
    lane = lax.broadcasted_iota(jnp.int32, block.shape, 1)
    return jnp.sum(jnp.where(lane == index, block, 0.0), axis=1, keepdims=True)


def encode(values):
    scale = jnp.max(jnp.abs(values), axis=1, keepdims=True)
    codes = jnp.floor(values * (CODE_TOP / jnp.maximum(scale, 1e-30)) + 0.5)
    return codes.astype(jnp.int32).astype(jnp.int16), scale * (1.0 / CODE_TOP)


def decode(codes):
    return codes.astype(jnp.int32).astype(jnp.float32)


def join_stats(top, total, scales):
    lane = lax.broadcasted_iota(jnp.int32, top.shape, 1)
    return jnp.where(lane < 16, top, jnp.where(lane < 32, pltpu.roll(total, 16, 1), scales))


def decode_kernel(
    served_ref, counts_ref, tail_ref, dest_ref, q_ref, lat_ref, own_ref, gain_ref, frequency_ref,
    out_ref, cache_ref,
    meta_ref, table,
    xbuf, lbuf, q_all, q_rows, partner, fresh, outgoing,
    states, state_m, state_l, o_codes, stats,
    relay_in, direct_in, merged, merged_in, stat_in, mstat, mstat_in,
    zcodes, zin, zstat, zstat_in, values, out_f32,
    send_x, recv_x, send_q, recv_q, send_page, recv_page, send_role, recv_role,
    send_y, recv_y, send_z, recv_z, local_sem,
):
    role = lax.axis_index("role")
    group = lax.axis_index("grp")
    me = lax.axis_index("dev")
    z = me // RING_Y
    y = me % RING_Y
    up = (y + 1) % RING_Y
    down = (y + 3) % RING_Y
    far = (y + 2) % RING_Y
    rows = 8 * OWNERS
    pages = own_ref.shape[0]
    at_prefill = role == 0

    def at(zz, yy):
        return (role, group, zz * RING_Y + yy)

    other_core = (1 - role, group, me)
    neighbours = {
        "up": at(z, up),
        "down": at(z, down),
        "in": at((z + 1) % RING_Z, y),
        "out": at((z + 7) % RING_Z, y),
    }
    shards = [(role, (group + k) % 4, me) for k in range(1, 4)]
    greet(everyone(role, group, z, y) + shards + [other_core])
    copies = []

    def push(src, dst, sends, recvs, index, target):
        copy = pltpu.make_async_remote_copy(
            src_ref=src, dst_ref=dst, send_sem=sends.at[index], recv_sem=recvs.at[index],
            device_id=target, device_id_type=MESH_IDS,
        )
        copy.start()
        copies.append(copy)
        return copy

    arriving, arriving_latents = [], []
    for k in (2, 1, 3):
        target = (role, (group + k) % 4, me)
        arriving.append(push(q_ref, xbuf.at[group], send_x, recv_x, 2 * k, target))
    exchange = push(own_ref, partner, send_role, recv_role, OWNERS, other_core)
    for k in (2, 1, 3):
        target = (role, (group + k) % 4, me)
        arriving_latents.append(push(lat_ref, lbuf.at[group], send_x, recv_x, 2 * k + 1, target))
    xbuf[group] = q_ref[...]
    lbuf[group] = lat_ref[...]

    def served(j):
        return served_ref[group * 12 + j]

    def context(j):
        return PAGE * (counts_ref[0, j] - 1) + tail_ref[0, j]

    run = 0
    for j in range(12):
        meta_ref[BEGIN + j] = (run - me + OWNERS - 1) // OWNERS
        run = run + counts_ref[0, j]
        meta_ref[END + j] = (run - me + OWNERS - 1) // OWNERS
        meta_ref[RUN_END + j] = run

    def describe(x, _):
        flat = x * OWNERS + me
        request = 0
        for j in range(11):
            request = request + (flat >= meta_ref[RUN_END + j]).astype(jnp.int32)
        meta_ref[REQUEST + x] = request
        meta_ref[VALID + x] = jnp.where(
            flat < meta_ref[RUN_END + request] - 1, PAGE, tail_ref[0, request]
        )
        meta_ref[SAME + x] = (x > meta_ref[BEGIN + request]).astype(jnp.int32)
        return 0

    lax.fori_loop(0, pages, describe, 0)

    def invert(t, _):
        page = -1
        for i in range(24):
            page = jnp.where(dest_ref[me, i] == 2 * t + role, i, page)
        meta_ref[INVERSE + t] = page
        return 0

    lax.fori_loop(0, OWNERS, invert, 0)
    frequency = frequency_ref[...]
    token = lax.broadcasted_iota(jnp.int32, (PAGE, 128), 0)

    def one_table(i, _):
        base = context(i // 2) + (me * 2 + i % 2) * PAGE
        table[i] = rope_table(base + token, frequency)
        return 0

    lax.fori_loop(0, pages, one_table, 0)
    new_base = context(jnp.minimum(me, 11)) + 2 * OWNERS * PAGE
    new_table = rope_table(new_base + token[:16] % 4, frequency)
    for copy in arriving:
        copy.wait_recv()

    def pick(index):
        pair = xbuf[index // 12, (index % 12) // 2].astype(jnp.float32)
        return jnp.where(index % 2 == 0, pair[:8], pair[8:])

    for p in range(6):
        both = jnp.concatenate([pick(served(2 * p)), pick(served(2 * p + 1))], axis=0)
        q_all[me, 16 * p : 16 * p + 16, :] = both.astype(jnp.bfloat16)

    def slot(dz, dy):
        return ((z - dz + 2 * RING_Z) % RING_Z) * RING_Y + (y - dy + 2 * RING_Y) % RING_Y

    waits = {}

    def send(half, dz, dy, to):
        span = pl.ds(48 * half, 48)
        place = slot(dz, dy)
        ndz = dz + {"in": 1, "out": -1}.get(to, 0)
        ndy = dy + {"up": 1, "down": -1}.get(to, 0)
        index = half * 32 + (ndz % RING_Z) * RING_Y + ndy % RING_Y
        block = q_all.at[place, span]
        push(block, block, send_q, recv_q, index, neighbours[to])
        here = q_all.at[slot(ndz, ndy), span]
        waits[half, ndz, ndy] = pltpu.make_async_remote_copy(
            src_ref=here, dst_ref=here, send_sem=send_q.at[index], recv_sem=recv_q.at[index],
            device_id=neighbours[to], device_id_type=MESH_IDS,
        )
        return (half, ndz, ndy)

    def z_steps(half, dz, dy):
        deep = 4 if (half == 0 or dy in (0, 1)) else 3
        steps = []
        if 0 <= dz < deep:
            steps.append("in")
        if 0 >= dz > deep - 7:
            steps.append("out")
        return steps

    def y_steps(half, dz, dy):
        if dy == 0:
            return ["up", "down"]
        if dy == 1 and (half == 1 or dz % 2 == 0):
            return ["up"]
        if dy == -1 and half == 0 and dz % 2 == 1:
            return ["down"]
        return []

    def forward(block):
        half, dz, dy = block
        if half == 0:
            steps = (z_steps(half, dz, dy) if dy == 0 else []) + y_steps(half, dz, dy)
        else:
            steps = (y_steps(half, dz, dy) if dz == 0 else []) + z_steps(half, dz, dy)
        return [send(half, dz, dy, to) for to in steps]

    def advance(frontier):
        later = []
        for block in frontier:
            waits[block].wait_recv()
            later = later + forward(block)
        return later

    frontier = forward((0, 0, 0)) + forward((1, 0, 0))

    exchange.wait_recv()
    gain = gain_ref[...]

    def finish(raw, turns):
        latent = raw[:, :LAT]
        mean_square = jnp.sum(latent * latent, axis=-1, keepdims=True) * (1.0 / LAT)
        normed = latent * lax.rsqrt(mean_square + epsilon) * gain
        rope = raw[:, LAT:]
        swapped = jnp.concatenate([rope[:, 32:], rope[:, :32]], axis=-1)
        turned = rope * turns[:, :64] + swapped * turns[:, 64:]
        return jnp.concatenate([normed, turned], axis=-1).astype(jnp.bfloat16)

    def one_page(i, _):
        raw = jnp.where(at_prefill, own_ref[i], partner[i]).astype(jnp.float32)
        fresh[i] = finish(raw, table[i])
        return 0

    third = pages // 3
    for part in range(3):
        lax.fori_loop(part * third, (part + 1) * third, one_page, 0)
        if part < 2:
            frontier = advance(frontier)

    def one_slot(t, _):
        page = meta_ref[INVERSE + t]
        found = fresh[jnp.maximum(page, 0)]
        outgoing[t] = jnp.where(page >= 0, found, jnp.zeros_like(found))
        return 0

    lax.fori_loop(0, OWNERS, one_slot, 0)
    frontier = advance(frontier)

    sent_pages = DISTANCES[:-1]
    landing = []
    over = []

    def send_pages(first, last):
        for i in range(first, last):
            dz, dy = sent_pages[i]
            there = ((z + dz) % RING_Z) * RING_Y + (y + dy) % RING_Y
            landing.append(
                push(
                    outgoing.at[there], cache_ref.at[me, role], send_page, recv_page, i,
                    (role, group, there),
                )
            )

    def hand_over(first, last):
        for i in range(first, last):
            dz, dy = sent_pages[i]
            landing[i].wait_recv()
            page = cache_ref.at[slot(dz, dy), role]
            over.append(push(page, page, send_role, recv_role, i, other_core))

    send_pages(0, EARLY)
    keep_own = pltpu.make_async_copy(outgoing.at[me], cache_ref.at[me, role], local_sem)
    keep_own.start()
    over.append(
        push(outgoing.at[me], cache_ref.at[me, role], send_role, recv_role, OWNERS - 1, other_core)
    )
    while frontier:
        frontier = advance(frontier)
    send_pages(EARLY, BEFORE_ATTENTION)

    def order_rows(p, _):
        for yy in range(RING_Y):
            blocks = [
                q_all[zz * RING_Y + yy, pl.ds(pl.multiple_of(16 * p, 16), 16), :].astype(jnp.float32)
                for zz in range(RING_Z)
            ]
            for jj in range(2):
                picked = jnp.concatenate([block[jj * 8 : jj * 8 + 8] for block in blocks], axis=0)
                q_rows[2 * p + jj, yy * 64 : yy * 64 + 64, :] = picked.astype(jnp.bfloat16)
        return 0

    lax.fori_loop(0, 6, order_rows, 0)

    lane = lax.broadcasted_iota(jnp.int32, (rows, 2 * PAGE), 1)
    low = lane < PAGE
    step_of_row = (lax.broadcasted_iota(jnp.int32, (rows, 2 * PAGE), 0) % 8) // 2

    def score(q, keys):
        s = lax.dot_general(q, keys, (((1,), (1,)), ((), ())), preferred_element_type=jnp.float32)
        return s * logit_scale_factor

    states[0] = jnp.zeros((rows, LAT), jnp.float32)
    state_m[0] = jnp.zeros((rows, 128), jnp.float32)
    state_l[0] = jnp.zeros((rows, 128), jnp.float32)
    page_lane = lax.broadcasted_iota(jnp.int32, (rows, PAGE), 1)

    def page_terms(x):
        request = meta_ref[REQUEST + x]
        keys = jnp.where(at_prefill, partner[x], own_ref[x])
        visible = page_lane < meta_ref[VALID + x]
        s = jnp.where(visible, score(q_rows[request], keys), lowest)
        m = jnp.max(s, axis=1, keepdims=True)
        e = jnp.where(visible, jnp.exp(s - m), 0.0)
        l = jnp.sum(e, axis=1, keepdims=True)
        o = jnp.dot(e.astype(jnp.bfloat16), keys[:, :LAT], preferred_element_type=jnp.float32)
        return m, l, o

    def wide(column_values):
        return jnp.broadcast_to(column_values, (rows, 128))

    def blend(left, a, right, b):
        tiles = [
            left[:, k : k + 128] * a + right[:, k : k + 128] * b for k in range(0, LAT, 128)
        ]
        return jnp.concatenate(tiles, axis=1)

    def chain(x, terms):
        m, l, o = terms
        same = meta_ref[SAME + x] == 1
        m = wide(m)
        m_before = jnp.where(same, state_m[x], lowest)
        m_now = jnp.maximum(m, m_before)
        carry = jnp.where(same, jnp.exp(m_before - m_now), 0.0)
        f = jnp.exp(m - m_now)
        state_m[x + 1] = m_now
        state_l[x + 1] = state_l[x] * carry + wide(l) * f
        states[x + 1] = blend(states[x], carry, o, f)

    def two_resident(i, _):
        terms = [page_terms(2 * i), page_terms(2 * i + 1)]
        chain(2 * i, terms[0])
        chain(2 * i + 1, terms[1])
        return 0

    lax.fori_loop(0, pages // 2, two_resident, 0)

    for copy in arriving_latents:
        copy.wait_recv()

    mine = served(jnp.minimum(me, 11))
    new_raw = lbuf[mine // 12, (mine % 12) // 4].astype(jnp.float32)
    new_keys = finish(new_raw, new_table)
    new_keys = jnp.concatenate(
        [new_keys, jnp.zeros((2 * PAGE - 16, KDIM), jnp.bfloat16)], axis=0
    )
    new_visible = (lane // 4 == mine % 4) & (lane % 4 <= step_of_row)

    def weigh(q, keys):
        s = score(q, keys)
        m1 = jnp.max(jnp.where(low, s, lowest), axis=1, keepdims=True)
        m2 = jnp.max(jnp.where(low, lowest, s), axis=1, keepdims=True)
        mb = jnp.where(low, m1, m2)
        e = jnp.exp(s - mb)
        m_now = jnp.maximum(m1, m2)
        f = jnp.exp(mb - m_now)
        l = jnp.sum(e * f, axis=1, keepdims=True)
        wide = e.astype(jnp.bfloat16).astype(jnp.float32) * f
        hi = wide.astype(jnp.bfloat16)
        lo = (wide - hi.astype(jnp.float32)).astype(jnp.bfloat16)
        v = keys[:, :LAT]
        o = jnp.dot(
            jnp.concatenate([hi, lo], axis=1),
            jnp.concatenate([v, v], axis=0),
            preferred_element_type=jnp.float32,
        )
        return m_now, l, o

    def whole_request(c, j):
        keys = fresh[pl.ds(2 * j, 2)].reshape(2 * PAGE, KDIM)
        m, l, o = weigh(q_rows[j], keys)
        last = meta_ref[END + j]
        has = meta_ref[END + j] > meta_ref[BEGIN + j]
        m = wide(m)
        m_state = jnp.where(has, state_m[last], lowest)
        m_now = jnp.maximum(m, m_state)
        f = jnp.exp(m - m_now)
        g = jnp.where(has, jnp.exp(m_state - m_now), 0.0)
        l_now = wide(l) * f + state_l[last] * g
        codes, scale = encode(blend(o, f, states[last], g))
        o_codes[:, j] = codes.reshape(RING_Y, rows // RING_Y, LAT)
        put_stats(c, j, m_now, l_now, scale)

        @pl.when(j == me)
        def _():
            s = jnp.where(new_visible, score(q_rows[j], new_keys), lowest)
            m_new = jnp.max(s, axis=1, keepdims=True)
            e = jnp.where(new_visible, jnp.exp(s - m_new), 0.0)
            l_new = jnp.sum(e, axis=1, keepdims=True)
            o_new = jnp.dot(
                e.astype(jnp.bfloat16), new_keys[:, :LAT], preferred_element_type=jnp.float32
            )
            m_new = wide(m_new)
            m_all = jnp.maximum(m_now, m_new)
            old = jnp.exp(m_now - m_all)
            fresh_part = jnp.exp(m_new - m_all)
            mixed = blend(blend(o, f, states[last], g), old, o_new, fresh_part)
            codes, scale = encode(mixed)
            o_codes[:, j] = codes.reshape(RING_Y, rows // RING_Y, LAT)
            put_stats(c, j, m_all, l_now * old + wide(l_new) * fresh_part, scale)

    def put_stats(c, j, m, l, scale):
        block = stats[c].reshape(rows, 128)
        block = jnp.where(lane == 16 + j, l, jnp.where(lane == 32 + j, scale, block))
        stats[c] = jnp.where(lane == j, m, block).reshape(RING_Y, rows // RING_Y, 128)

    ways = (up, down)
    stat_far, stat_near, relayed, direct = {}, {}, {}, {}
    def attend(c):
        stats[c] = jnp.zeros((RING_Y, rows // RING_Y, 128), jnp.float32)

        def two_requests(i, _, c=c):
            whole_request(c, HALF * c + i)
            whole_request(c, 6 + HALF * c + i)
            return 0

        lax.fori_loop(0, HALF, two_requests, 0)
        for way, ahead in enumerate(ways):
            base = 6 * way + HALF * c
            first = 8 * c + 2 * way
            stat_far[c, way] = push(
                stats.at[c, far], stat_in.at[c, 2 * way], send_y, recv_y, first, at(z, ahead)
            )
            relayed[c, way] = push(
                o_codes.at[far, pl.ds(base, HALF)], relay_in.at[way, c], send_y, recv_y,
                first + 1, at(z, ahead),
            )
        for way, ahead in enumerate(ways):
            base = 6 * (1 - way) + HALF * c
            first = 8 * c + 4 + 2 * way
            stat_near[c, way] = push(
                stats.at[c, ahead], stat_in.at[c, 2 * way + 1], send_y, recv_y, first, at(z, ahead)
            )
            direct[c, way] = push(
                o_codes.at[ahead, pl.ds(base, HALF)], direct_in.at[way, c], send_y, recv_y,
                first + 1, at(z, ahead),
            )

    passed, passed_stat = {}, {}
    def relay(c):
        for way, ahead in enumerate(ways):
            stat_far[c, way].wait_recv()
            relayed[c, way].wait_recv()
            top, total, weights = merge_stats([stat_in[c, 2 * way], stats[c, ahead]])
            base = 6 * way + HALF * c

            def relay_one(i, scales, way=way, c=c, base=base, ahead=ahead, weights=weights):
                mixed = decode(relay_in[way, c, i]) * column(weights[0], base + i)
                mixed = mixed + decode(o_codes[ahead, base + i]) * column(weights[1], base + i)
                codes, scale = encode(mixed)
                merged[way, c, i] = codes
                at_lane = lax.broadcasted_iota(jnp.int32, scales.shape, 1)
                return jnp.where(at_lane == 32 + base + i, scale, scales)

            scales = lax.fori_loop(0, HALF, relay_one, jnp.zeros_like(top))
            mstat[way, c] = join_stats(top, total, scales)
            first = 8 * CHUNKS + 4 * c + 2 * way
            passed[c, way] = push(
                merged.at[way, c], merged_in.at[way, c], send_y, recv_y, first, at(z, ahead)
            )
            passed_stat[c, way] = push(
                mstat.at[way, c], mstat_in.at[way, c], send_y, recv_y, first + 1, at(z, ahead)
            )

    arrivals = {}

    def land(c):
        merged_stats = []
        for way in range(2):
            stat_near[c, 1 - way].wait_recv()
            passed_stat[c, way].wait_recv()
            passed[c, way].wait_recv()
            direct[c, 1 - way].wait_recv()
            merged_stats.append(
                merge_stats([stats[c, y], mstat_in[way, c], stat_in[c, 2 * (1 - way) + 1]])
            )
        small = lax.broadcasted_iota(jnp.int32, (64, 128), 1)
        scales = jnp.zeros((64, 128), jnp.float32)
        for way in range(2):
            base = 6 * way + HALF * c
            weights = merged_stats[way][2]

            def land_one(i, scales, way=way, c=c, base=base, weights=weights):
                mixed = decode(o_codes[y, base + i]) * column(weights[0], base + i)
                mixed = mixed + decode(merged_in[way, c, i]) * column(weights[1], base + i)
                mixed = mixed + decode(direct_in[1 - way, c, i]) * column(weights[2], base + i)
                scale = jnp.maximum(jnp.max(jnp.abs(mixed), axis=1, keepdims=True), 1e-30)
                values[way * HALF + i] = jnp.floor(mixed * (CODE_TOP / scale) + 0.5)
                return jnp.where(small == 32 + base + i, scale * (1.0 / CODE_TOP), scales)

            scales = lax.fori_loop(0, HALF, land_one, scales)
        use_up = (small % 16) < 6
        top = jnp.where(use_up, merged_stats[0][0], merged_stats[1][0])
        total = jnp.where(use_up, merged_stats[0][1], merged_stats[1][1])
        zstat[c] = join_stats(top, total, scales)

        def split_one(zz, _, c=c):
            part = values[:, pl.ds(pl.multiple_of(zz * 8, 8), 8), :]
            part = part.reshape(2 * HALF * 8, LAT)
            zcodes[c, zz] = part.astype(jnp.int32).astype(jnp.int16)
            return 0

        lax.fori_loop(0, RING_Z, split_one, 0)
        for k in (4, 3, 5, 2, 6, 1, 7):
            there = (z + k) % RING_Z
            index = 2 * (c * RING_Z + k)
            arrivals[c, k] = (
                push(
                    zstat.at[c, pl.ds(there * 8, 8)], zstat_in.at[c, k], send_z, recv_z, index + 1,
                    at(there, y),
                ),
                push(zcodes.at[c, there], zin.at[c, k], send_z, recv_z, index, at(there, y)),
            )

    for c in range(CHUNKS):
        attend(c)
        if c >= 1:
            relay(c - 1)
    send_pages(BEFORE_ATTENTION, len(sent_pages))
    relay(CHUNKS - 1)
    hand_over(0, 8)
    for c in range(CHUNKS):
        land(c)
    hand_over(8, len(sent_pages))
    for c in range(CHUNKS):
        for k in range(1, RING_Z):
            for copy in arrivals[c, k]:
                copy.wait_recv()
        finished = []
        blocks = [zstat[c, pl.ds(pl.multiple_of(z * 8, 8), 8), :]]
        blocks = blocks + [zstat_in[c, k] for k in range(1, RING_Z)]
        top, total, weights = merge_stats(blocks)
        for way in range(2):
            base = 6 * way + HALF * c
            sums = [1.0 / column(total, base + i) for i in range(HALF)]
            mixed = None
            for k in range(RING_Z):
                codes = zcodes.at[c, z] if k == 0 else zin.at[c, k]
                part = decode(codes[...])[way * HALF * 8 : (way + 1) * HALF * 8]
                factor = jnp.concatenate(
                    [column(weights[k], base + i) * sums[i] for i in range(HALF)], axis=0
                )
                mixed = part * factor if mixed is None else mixed + part * factor
            finished.append((base, mixed))
        for base, mixed in finished:
            out_f32[base * 8 : (base + HALF) * 8, :] = mixed
    out_ref[...] = out_f32[...].astype(jnp.bfloat16)
    keep_own.wait()
    for copy in over:
        copy.wait_recv()
    for copy in copies:
        copy.wait_send()


def decode_step(served, counts, tails, dest, queries, latents, own, gain, frequency):
    smem = pl.BlockSpec(memory_space=pltpu.SMEM)
    vmem = pl.BlockSpec(memory_space=pltpu.VMEM)
    hbm = pl.BlockSpec(memory_space=pl.ANY)
    pages = own.shape[0]
    rows = 8 * OWNERS
    half = (2, CHUNKS, HALF, 64, LAT)
    bf16, f32, i16 = jnp.bfloat16, jnp.float32, jnp.int16
    dma = pltpu.SemaphoreType.DMA
    return pl.pallas_call(
        decode_kernel,
        out_shape=(
            jax.ShapeDtypeStruct((96, LAT), bf16),
            jax.ShapeDtypeStruct((OWNERS, 2, PAGE, KDIM), bf16),
        ),
        in_specs=[smem, smem, smem, smem, vmem, vmem, vmem, vmem, vmem],
        out_specs=(vmem, hbm),
        scratch_shapes=[
            pltpu.SMEM((144,), jnp.int32),
            pltpu.VMEM((pages, PAGE, 128), f32),
            pltpu.VMEM((4, 6, 16, KDIM), bf16),
            pltpu.VMEM((4, 3, 16, KDIM), bf16),
            pltpu.VMEM((OWNERS, 96, KDIM), bf16),
            pltpu.VMEM((12, rows, KDIM), bf16),
            pltpu.VMEM((pages, PAGE, KDIM), bf16),
            pltpu.VMEM((pages, PAGE, KDIM), bf16),
            pltpu.VMEM((OWNERS, PAGE, KDIM), bf16),
            pltpu.VMEM((pages + 1, rows, LAT), f32),
            pltpu.VMEM((pages + 1, rows, 128), f32),
            pltpu.VMEM((pages + 1, rows, 128), f32),
            pltpu.VMEM((RING_Y, 12, rows // RING_Y, LAT), i16),
            pltpu.VMEM((CHUNKS, RING_Y, rows // RING_Y, 128), f32),
            pltpu.VMEM(half, i16),
            pltpu.VMEM(half, i16),
            pltpu.VMEM(half, i16),
            pltpu.VMEM(half, i16),
            pltpu.VMEM((CHUNKS, 4, 64, 128), f32),
            pltpu.VMEM((2, CHUNKS, 64, 128), f32),
            pltpu.VMEM((2, CHUNKS, 64, 128), f32),
            pltpu.VMEM((CHUNKS, RING_Z, 16 * HALF, LAT), i16),
            pltpu.VMEM((CHUNKS, RING_Z, 16 * HALF, LAT), i16),
            pltpu.VMEM((CHUNKS, 64, 128), f32),
            pltpu.VMEM((CHUNKS, RING_Z, 8, 128), f32),
            pltpu.VMEM((2 * HALF, 64, LAT), f32),
            pltpu.VMEM((96, LAT), f32),
            dma((8,)),
            dma((8,)),
            dma((64,)),
            dma((64,)),
            dma((OWNERS,)),
            dma((OWNERS,)),
            dma((OWNERS + 1,)),
            dma((OWNERS + 1,)),
            dma((12 * CHUNKS,)),
            dma((12 * CHUNKS,)),
            dma((2 * CHUNKS * RING_Z,)),
            dma((2 * CHUNKS * RING_Z,)),
            dma,
        ],
        compiler_params=pltpu.CompilerParams(
            vmem_limit_bytes=VMEM_LIMIT, collective_id=1, has_side_effects=True
        ),
        cost_estimate=pl.CostEstimate(
            flops=2_000_000_000, bytes_accessed=100_000_000, transcendentals=0
        ),
        name="decode_step",
    )(served, counts, tails, dest, queries, latents, own, gain.reshape(1, LAT), frequency)


def per_device(
    pool_pages,
    kv_gain,
    queries,
    decode_latent,
    served_request,
    resident_pages,
    resident_tail,
    page_dest,
):
    own = pool_pages[0, 0, 0]
    req_grp = resident_pages.shape[1]
    steps = queries.shape[1]
    heads_here = queries.shape[2]
    frequency = 10000.0 ** (-(jnp.arange(128) % 32).astype(jnp.float32) / 32)
    attention, received = decode_step(
        served_request, resident_pages, resident_tail, page_dest[0],
        queries.reshape(6, 16, KDIM), decode_latent.reshape(3, 16, KDIM), own, kv_gain,
        frequency.reshape(1, 128),
    )
    attention = attention.reshape(req_grp, steps, heads_here, LAT)
    received = received.reshape(1, 1, 2 * OWNERS, PAGE, KDIM)
    return (attention, received)


def solution(mesh):
    in_specs = (
        P("role", "grp", "dev", None, None, None),
        P(),
        P("grp", None, ("role", "dev"), None),
        P("grp", None, None),
        P(),
        P("grp", None),
        P("grp", None),
        P("grp", None, None),
    )
    out_specs = (P("grp", None, ("role", "dev"), None), P("grp", "dev", None, None, None))
    return jax.shard_map(
        per_device, mesh=mesh, in_specs=in_specs, out_specs=out_specs, check_vma=False
    )
```
